256 devices in a mesh: dp: 8 (over z_lo, x), seq: 32 (over z_hi, y, core).
Axes of the slice: x: 4, y: 4, z: 8 (z_hi: 4, z_lo: 2; z = z_hi * 2 + z_lo), core: 2. Of those that a mesh axis runs over, the one named last changes fastest.
Arguments:
- tokens: bfloat16 [8, 128, 256, 768], P('dp', 'seq'), may hold values from -6 to 6
- grad_out: bfloat16 [8, 128, 256, 768], P('dp', 'seq'), may hold values from -6 to 6
- right_blocks: bfloat16 [128, 256, 256], P('seq'), may hold values from -0.375 to 0.375
- left_blocks: bfloat16 [256, 128, 128], P('seq'), may hold values from -0.5 to 0.5
- in_weight: bfloat16 [768, 768], replicated, may hold values from -0.21875 to 0.21875
Outputs:
- mixed: bfloat16 [8, 128, 256, 768], P('dp', 'seq')
- grad_tokens: bfloat16 [8, 128, 256, 768], P('dp', 'seq')
- grad_left: bfloat16 [256, 128, 128], P('seq')
- grad_right: bfloat16 [128, 256, 256], P('seq')
- grad_weight: bfloat16 [768, 768], replicated
The draws below stay inside these ranges and needn't reach their ends.
All inputs are finite; a program needn't handle non-finite values.
Results may differ from the reference program's by a relative error of at most 0.007.
Values may be sent and summed in bfloat16 or wider, within the bound.
No kernel may reach another device: no remote copies, remote signals or barrier semaphores. Data moves between devices by JAX's collectives and lax.ppermute only.
A program may use at most 128 MiB of HBM per device.

```python
import jax
import jax.numpy as jnp
from jax import lax

A = 128
B = 256
D = 768
DOCS = 8


def levels(own_key, dims, split, least, high):
    gain = 1.0
    for dim, blocks in split:
        draws = jax.random.uniform(jax.random.fold_in(jax.random.fold_in(own_key, 6), dim), (blocks,), jnp.float32, least / len(split), high / len(split))
        gain = gain * jnp.repeat(jnp.exp(draws), dims[dim] // blocks).reshape((-1,) + (1,) * (len(dims) - 1 - dim))
    return gain


def scatter_about(key, shape, deviation, reach, shards=(), dtype=jnp.bfloat16):
    values = deviation * jax.random.normal(key, shape, jnp.float32)
    if shards:
        values = values * levels(key, shape, shards, -0.22, 0.18)
    return jnp.clip(values, -reach, reach).astype(dtype)


def setup_inputs(seed: int = 0) -> dict:
    seeds = jax.random.split(jax.random.key(seed), 6)
    return {
        "tokens": scatter_about(seeds[0], (DOCS, A, B, D), 1.0, 6.0, ((0, 8), (1, 32))),
        "grad_out": scatter_about(seeds[1], (DOCS, A, B, D), 1.0, 6.0, ((0, 8), (1, 32))),
        "right_blocks": scatter_about(seeds[2], (A, B, B), B ** -0.5, 0.375, ((0, 32),)),
        "left_blocks": scatter_about(seeds[3], (B, A, A), A ** -0.5, 0.5, ((0, 32),)),
        "in_weight": scatter_about(seeds[4], (D, D), D ** -0.5, 0.21875),
    }


def per_document(tokens, grad_out, right_blocks, left_blocks, in_weight):
    right_wide = right_blocks.astype(jnp.float32)
    left_wide = left_blocks.astype(jnp.float32)
    flat_tokens = tokens.reshape(-1, D)
    projected = jnp.dot(flat_tokens, in_weight, preferred_element_type=jnp.float32).astype(jnp.bfloat16).reshape(A, B, D)
    section_one = jnp.einsum('aeb,abd->aed', right_wide, projected.astype(jnp.float32)).astype(jnp.bfloat16)
    section_two = jnp.einsum('jxa,ajd->xjd', left_wide, section_one.astype(jnp.float32)).astype(jnp.bfloat16)
    mixed = (section_two.astype(jnp.float32) * tokens.astype(jnp.float32)).astype(jnp.bfloat16)
    grad_two = (grad_out.astype(jnp.float32) * tokens.astype(jnp.float32)).astype(jnp.bfloat16)
    grad_left = jnp.einsum('xjd,ajd->jxa', grad_two.astype(jnp.float32), section_one.astype(jnp.float32))
    grad_one = jnp.einsum('jxa,xjd->ajd', left_wide, grad_two.astype(jnp.float32)).astype(jnp.bfloat16)
    grad_right = jnp.einsum('aed,abd->aeb', grad_one.astype(jnp.float32), projected.astype(jnp.float32))
    grad_proj = jnp.einsum('aeb,aed->abd', right_wide, grad_one.astype(jnp.float32)).astype(jnp.bfloat16)
    flat_proj = grad_proj.reshape(-1, D)
    grad_weight = jnp.dot(flat_tokens.T, flat_proj, preferred_element_type=jnp.float32)
    back_proj = jnp.dot(flat_proj, in_weight.T, preferred_element_type=jnp.float32).reshape(A, B, D)
    grad_tokens = (grad_out.astype(jnp.float32) * section_two.astype(jnp.float32) + back_proj).astype(jnp.bfloat16)
    return mixed, grad_tokens, grad_left, grad_right, grad_weight


def reference(tokens, grad_out, right_blocks, left_blocks, in_weight):
    def step_over(carry, pair):
        mixed, grad_tokens, grad_left, grad_right, grad_weight = per_document(pair[0], pair[1], right_blocks, left_blocks, in_weight)
        carry = (carry[0] + grad_left, carry[1] + grad_right, carry[2] + grad_weight)
        return carry, (mixed, grad_tokens)

    start = (jnp.zeros((B, A, A), jnp.float32), jnp.zeros((A, B, B), jnp.float32), jnp.zeros((D, D), jnp.float32))
    totals, outputs = lax.scan(step_over, start, (tokens, grad_out))
    return outputs[0], outputs[1], totals[0].astype(jnp.bfloat16), totals[1].astype(jnp.bfloat16), totals[2].astype(jnp.bfloat16)
```

```python
import jax
import jax.numpy as jnp
from jax import lax
from jax.sharding import Mesh, PartitionSpec as P

F32 = jnp.float32
BF16 = jnp.bfloat16
CHIPS = ("zh", "y")


def exchange(v):
    return lax.all_to_all(v, CHIPS, split_axis=0, concat_axis=0, tiled=True)


def swap_halves(v, axis):
    core = lax.axis_index("c")
    mine = lax.dynamic_index_in_dim(v, core, axis, keepdims=False)
    theirs = lax.dynamic_index_in_dim(v, 1 - core, axis, keepdims=False)
    got = lax.ppermute(theirs, "c", [(0, 1), (1, 0)])
    return jnp.where(core == 0, mine, got), jnp.where(core == 0, got, mine)


def split_rows(rows):
    a, b, d = rows.shape
    return rows.reshape(a, 16, b // 16, d).transpose(1, 0, 2, 3)


def join_rows(parts):
    chips, a, b, d = parts.shape
    return parts.transpose(1, 0, 2, 3).reshape(a, chips * b, d)


def own_columns(parts):
    chips, a, b, d = parts.shape
    first, second = swap_halves(parts.reshape(chips, a, 2, b // 2, d), 2)
    return jnp.stack([first, second], axis=1).reshape(chips * 2 * a, b // 2, d)


def split_columns(cols):
    a, b, d = cols.shape
    first, second = swap_halves(cols.reshape(16, 2, a // 32, b, d), 1)
    return jnp.concatenate([first, second], axis=2)


def scatter_sum(part, axis, size):
    me = lax.axis_index(axis)
    chunks = part.reshape((size, part.shape[0] // size) + part.shape[1:])
    total = lax.dynamic_index_in_dim(chunks, me, 0, keepdims=False)
    for k in range(1, size):
        away = lax.dynamic_index_in_dim(chunks, (me + k) % size, 0, keepdims=False)
        total = total + lax.ppermute(away, axis, [(i, (i + k) % size) for i in range(size)])
    return total


def gather(part, axis, size):
    me = lax.axis_index(axis)
    got = [part]
    for k in range(1, size):
        got.append(lax.ppermute(part, axis, [(i, (i + k) % size) for i in range(size)]))
    got = jnp.stack(got)
    return jnp.concatenate([lax.dynamic_index_in_dim(got, (me - i) % size, 0, keepdims=False) for i in range(size)])


SIZES = {"zl": 2, "x": 4, "zh": 4, "y": 4, "c": 2}


def sum_over(part, axes):
    for axis in axes:
        part = scatter_sum(part, axis, SIZES[axis])
    part = part.astype(BF16)
    for axis in reversed(axes):
        part = gather(part, axis, SIZES[axis])
    return part


def after(v, *others):
    return lax.optimization_barrier((v,) + others)[0]


def on_device(tokens, grad_out, right_blocks, left_blocks, in_weight):
    tokens, grad_out = tokens[0], grad_out[0]
    grad_two = (grad_out.astype(F32) * tokens.astype(F32)).astype(BF16)
    grad_parts = exchange(split_rows(grad_two))

    token_one = jnp.einsum("aeb,abc->aec", right_blocks, tokens, preferred_element_type=F32).astype(BF16)
    projected = jnp.einsum("abc,cd->abd", tokens, in_weight, preferred_element_type=F32).astype(BF16)
    token_split = split_rows(token_one)
    token_split, projected, grad_parts = lax.optimization_barrier((token_split, projected, grad_parts))
    token_parts = exchange(token_split)

    grad_cols = own_columns(grad_parts)
    one_cols = jnp.einsum("jxa,xjd->ajd", left_blocks, grad_cols, preferred_element_type=F32).astype(BF16)
    one_split = split_columns(one_cols)
    one_split, grad_cols, one_cols, token_parts = lax.optimization_barrier((one_split, grad_cols, one_cols, token_parts))
    one_parts = exchange(one_split)

    token_cols = own_columns(token_parts)
    columns = jnp.einsum("ajc,cd->ajd", token_cols, in_weight, preferred_element_type=F32).astype(BF16)
    two_cols = jnp.einsum("jxa,ajd->xjd", left_blocks, columns, preferred_element_type=F32).astype(BF16)
    two_split = split_columns(two_cols)
    weight_part = jnp.einsum("ajc,ajd->cd", token_cols, one_cols, preferred_element_type=F32)
    left_part = jnp.einsum("xjd,ajd->jxa", grad_cols, columns, preferred_element_type=F32)
    two_split, weight_part, left_part, one_parts = lax.optimization_barrier((two_split, weight_part, left_part, one_parts))
    two_parts = exchange(two_split)

    grad_weight = sum_over(weight_part, ("c", "x", "zl", "y", "zh"))
    grad_left = sum_over(left_part, ("x", "zl"))
    grad_one = join_rows(one_parts)
    right_part = jnp.einsum("aed,abd->aeb", grad_one, projected, preferred_element_type=F32)
    grad_right = sum_over(right_part.reshape(-1, right_part.shape[2]), ("x", "zl")).reshape(right_part.shape)
    grad_proj = jnp.einsum("aeb,aed->abd", right_blocks, grad_one, preferred_element_type=F32).astype(BF16)
    back_proj = jnp.einsum("abd,cd->abc", grad_proj, in_weight, preferred_element_type=F32)
    grad_weight, grad_left, grad_right, back_proj, two_parts = lax.optimization_barrier((grad_weight, grad_left, grad_right, back_proj, two_parts))
    section_two = join_rows(two_parts)
    mixed = (section_two.astype(F32) * tokens.astype(F32)).astype(BF16)
    grad_tokens = (grad_out.astype(F32) * section_two.astype(F32) + back_proj).astype(BF16)
    return mixed[None], grad_tokens[None], grad_left, grad_right, grad_weight


def solution(mesh):
    fine = Mesh(mesh.devices.reshape(2, 4, 4, 4, 2), ("zl", "x", "zh", "y", "c"))
    dp, seq = ("zl", "x"), ("zh", "y", "c")
    rows = P(dp, seq, None, None)
    blocks = P(seq, None, None)
    return jax.shard_map(
        on_device,
        mesh=fine,
        in_specs=(rows, rows, blocks, blocks, P()),
        out_specs=(rows, rows, blocks, blocks, P()),
        check_vma=False,
    )
```

```python
import jax
import jax.numpy as jnp
from jax import lax
from jax.experimental import pallas as pl
from jax.experimental.pallas import tpu as pltpu
from jax.sharding import Mesh, PartitionSpec as P

F32 = jnp.float32
BF16 = jnp.bfloat16
CHIPS = ("zh", "y")
SIZES = {"zl": 2, "x": 4, "zh": 4, "y": 4, "c": 2}

LA, LJ, NCHIP, A, B, D = 4, 8, 16, 128, 256, 768
PARTS = jax.ShapeDtypeStruct((NCHIP, 2, LA * LJ, D), BF16)
WR, WCH = 576, 48
TWO = jax.ShapeDtypeStruct((NCHIP, 384 + WCH, 128), BF16)
VMEM = pl.BlockSpec(memory_space=pltpu.VMEM)
SMEM = pl.BlockSpec(memory_space=pltpu.SMEM)


def params(mib):
    return pltpu.CompilerParams(vmem_limit_bytes=mib * 1024 * 1024)


def cost(flops=1000, nbytes=1000):
    return pl.CostEstimate(flops=flops, bytes_accessed=nbytes, transcendentals=0)


def dot(a, b, ca, cb):
    return lax.dot_general(a, b, (((ca,), (cb,)), ((), ())), preferred_element_type=F32)


def grad_two_kernel(t_ref, g_ref, o_ref):
    for i in range(4):
        rows = pl.ds(i * 16, 16)
        v = t_ref[:, rows, :].astype(F32) * g_ref[:, rows, :].astype(F32)
        v = v.reshape(LA, 2, LJ, D)
        for core in range(2):
            o_ref[i, core] = v[:, core].reshape(LA * LJ, D).astype(BF16)


def grad_two_parts(tokens, grad_out):
    rows = pl.BlockSpec((LA, 64, D), lambda i: (0, i, 0))
    return pl.pallas_call(
        grad_two_kernel,
        grid=(4,),
        in_specs=[rows, rows],
        out_specs=pl.BlockSpec((4, 2, LA * LJ, D), lambda i: (i, 0, 0, 0)),
        out_shape=PARTS,
        compiler_params=params(60),
        name="grad_two",
    )(tokens, grad_out)


COLUMNS = pltpu.VMEM((6, A * LJ, 128), F32)


def put_rows(x_ref, rows, v):
    for k in range(6):
        x_ref[k, rows, :] = v[:, k * 128:(k + 1) * 128]


def get_rows(x_ref, rows):
    return jnp.concatenate([x_ref[k, rows, :] for k in range(6)], axis=1)


def to_parts(x_ref, o_ref):
    @pl.loop(0, NCHIP)
    def _(i):
        for core in range(2):
            o_ref[i, core] = get_rows(x_ref, pl.ds(i * 64 + core * 32, 32)).astype(BF16)


def front_kernel(t_ref, r_ref, w_ref, o_ref, p_ref, x_ref):
    for a in range(LA):
        t = t_ref[a]
        one = dot(r_ref[a], t, 1, 0)
        x_ref[:, pl.ds(a * LJ, LJ), :] = one.reshape(32, LJ, D)
        p_ref[a] = dot(t, w_ref[...], 1, 0).astype(BF16)

    @pl.loop(0, NCHIP)
    def _(i):
        o_ref[i] = x_ref[pl.ds(i * 2, 2)].astype(BF16)


def front(tokens, right_blocks, in_weight):
    return pl.pallas_call(
        front_kernel,
        in_specs=[VMEM] * 3,
        out_specs=[VMEM] * 2,
        out_shape=[PARTS, jax.ShapeDtypeStruct((LA, B, D), BF16)],
        scratch_shapes=[pltpu.VMEM((32, LA * LJ, D), F32)],
        compiler_params=params(18),
        cost_estimate=cost(),
        name="front",
    )(tokens, right_blocks, in_weight)


def load_columns(core, own_ref, other_ref, x_ref):
    @pl.loop(0, NCHIP)
    def _(i):
        put_rows(x_ref, pl.ds(i * 64 + core * 32, 32), own_ref[i, core].astype(F32))
        put_rows(x_ref, pl.ds(i * 64 + (1 - core) * 32, 32), other_ref[i, core].astype(F32))


def one_kernel(core_ref, own_ref, other_ref, l_ref, o_ref, gj_ref, oj_ref, x_ref):
    load_columns(core_ref[0], own_ref, other_ref, x_ref)
    for j in range(LJ):
        at = pl.ds(j, A, stride=LJ)
        g = get_rows(x_ref, at).astype(BF16)
        one = dot(l_ref[j], g, 0, 0)
        gj_ref[j] = g
        oj_ref[j] = one.astype(BF16)
        put_rows(x_ref, at, one)
    to_parts(x_ref, o_ref)


def grad_one_columns(core, own, other, left_blocks):
    by_j = jax.ShapeDtypeStruct((LJ, A, D), BF16)
    return pl.pallas_call(
        one_kernel,
        in_specs=[SMEM] + [VMEM] * 3,
        out_specs=[VMEM] * 3,
        out_shape=[PARTS, by_j, by_j],
        scratch_shapes=[COLUMNS],
        compiler_params=params(18),
        cost_estimate=cost(),
        name="grad_one_columns",
    )(core, own, other, left_blocks)


def weight_kernel(core_ref, own_ref, other_ref, oj_ref, t_ref, mine_ref, theirs_ref, x_ref):
    core = core_ref[0]
    load_columns(core, own_ref, other_ref, x_ref)
    for j in range(LJ):
        t_ref[pl.ds(j * A, A), :] = get_rows(x_ref, pl.ds(j, A, stride=LJ)).astype(BF16)
    for half, out in ((1 - core, theirs_ref), (core, mine_ref)):
        t = t_ref[:, pl.ds(pl.multiple_of(half * 384, 128), 384)]
        part = dot(t, oj_ref[...].reshape(A * LJ, D), 0, 0)
        for q in range(4):
            for k in range(6):
                piece = part[q * 96:(q + 1) * 96, k * 128:(k + 1) * 128]
                out[q, pl.ds(k * 96, 96), :] = piece.astype(out.dtype)


def weight_grad(core, own, other, by_j_one):
    half = (4, WR, 128)
    return pl.pallas_call(
        weight_kernel,
        in_specs=[SMEM] + [VMEM] * 3,
        out_specs=[VMEM] * 3,
        out_shape=[
            jax.ShapeDtypeStruct((A * LJ, D), BF16),
            jax.ShapeDtypeStruct(half, F32),
            jax.ShapeDtypeStruct(half, BF16),
        ],
        scratch_shapes=[COLUMNS],
        compiler_params=params(18),
        cost_estimate=cost(),
        name="weight_grad",
    )(core, own, other, by_j_one)


def two_kernel(t_ref, w_ref, l_ref, gj_ref, o_ref, lp_ref, x_ref, s_ref):
    @pl.loop(0, 4)
    def _(i):
        rows = pl.ds(i * 256, 256)
        s_ref[rows, :] = dot(t_ref[rows, :], w_ref[...], 1, 0).astype(BF16)

    for j in range(LJ):
        v = s_ref[pl.ds(j * A, A), :]
        lp_ref[j] = dot(gj_ref[j], v, 1, 1)
        put_rows(x_ref, pl.ds(j, A, stride=LJ), dot(l_ref[j], v, 1, 0))

    @pl.loop(0, NCHIP)
    def _(i):
        for c in range(2):
            for k in range(6):
                o_ref[i, c, pl.ds(k * 32, 32), :] = x_ref[k, pl.ds(i * 64 + c * 32, 32), :].astype(BF16)


def two_columns(by_j_token, in_weight, left_blocks, by_j_grad):
    return pl.pallas_call(
        two_kernel,
        in_specs=[VMEM] * 4,
        out_specs=[VMEM] * 2,
        out_shape=[
            jax.ShapeDtypeStruct((NCHIP, 2, 192, 128), BF16),
            jax.ShapeDtypeStruct((LJ, A, A), F32),
        ],
        scratch_shapes=[COLUMNS, pltpu.VMEM((A * LJ, D), BF16)],
        compiler_params=params(18),
        cost_estimate=cost(),
        name="two_columns",
    )(by_j_token, in_weight, left_blocks, by_j_grad)


def spread_kernel(x_index_ref, mine_ref, got_ref, own_ref, *send_refs):
    x = x_index_ref[0]
    for k in range(4):
        q = lax.rem(x + k, 4)
        out = own_ref if k == 0 else send_refs[k - 1]
        out[...] = (mine_ref[q] + got_ref[q].astype(F32)).astype(out.dtype)


def spread(x_index, mine, got):
    return pl.pallas_call(
        spread_kernel,
        in_specs=[SMEM] + [VMEM] * 2,
        out_specs=[VMEM] * 4,
        out_shape=[jax.ShapeDtypeStruct((WR, 128), F32)] + [jax.ShapeDtypeStruct((WR, 128), BF16)] * 3,
        compiler_params=params(8),
        cost_estimate=cost(),
        name="spread",
    )(x_index, mine, got)


def join_two_kernel(core_ref, own_ref, other_ref, sum_ref, a_ref, b_ref, c_ref, o_ref, w_ref):
    core = core_ref[0]
    w = (sum_ref[...] + a_ref[...].astype(F32)) + (b_ref[...].astype(F32) + c_ref[...].astype(F32))
    w_ref[...] = w.astype(BF16)
    mine = pl.ds(pl.multiple_of(core * 192, 16), 192)
    theirs = pl.ds(pl.multiple_of((1 - core) * 192, 16), 192)

    @pl.loop(0, NCHIP)
    def _(i):
        o_ref[i, mine, :] = own_ref[i, core]
        o_ref[i, theirs, :] = other_ref[i, core]

    for i in range(NCHIP):
        chunk = w_ref[pl.ds(i * WCH, WCH), :] if i < WR // WCH else jnp.zeros((WCH, 128), BF16)
        o_ref[i, pl.ds(384, WCH), :] = chunk


def join_two(core, own, other, total, got):
    return pl.pallas_call(
        join_two_kernel,
        in_specs=[SMEM] + [VMEM] * 6,
        out_specs=VMEM,
        out_shape=TWO,
        scratch_shapes=[pltpu.VMEM((WR, 128), BF16)],
        compiler_params=params(14),
        cost_estimate=cost(),
        name="join_two",
    )(core, own, other, total, *got)


def weight_sum_kernel(p_ref, o_ref):
    total = p_ref[0].astype(F32)
    for i in range(1, NCHIP):
        total = total + p_ref[i].astype(F32)
    o_ref[...] = total


def weight_sum(two_parts):
    return pl.pallas_call(
        weight_sum_kernel,
        grid=(1,),
        in_specs=[pl.BlockSpec((NCHIP, WCH, 128), lambda i: (0, 384 // WCH, 0))],
        out_specs=pl.BlockSpec((WCH, 128), lambda i: (0, 0)),
        out_shape=jax.ShapeDtypeStruct((WCH, 128), F32),
        compiler_params=params(6),
        cost_estimate=cost(),
        name="weight_sum",
    )(two_parts)


def blocks_kernel(x_index_ref, own_ref, a_ref, b_ref, c_ref, l_ref, r_ref):
    for k, ref in enumerate((own_ref, a_ref, b_ref, c_ref)):
        q = lax.rem(x_index_ref[0] + 4 - k, 4)
        for h in range(2):
            l_ref[q * 2 + h] = ref[pl.ds(h * A, A), :]
            r_ref[q, :, pl.ds(h * 128, 128)] = ref[pl.ds(2 * A + h * B, B), :]


def place_blocks(x_index, pieces):
    return pl.pallas_call(
        blocks_kernel,
        in_specs=[SMEM] + [VMEM] * 4,
        out_specs=[VMEM] * 2,
        out_shape=[jax.ShapeDtypeStruct((LJ, A, A), BF16), jax.ShapeDtypeStruct((LA, B, B), BF16)],
        compiler_params=params(6),
        cost_estimate=cost(),
        name="place_blocks",
    )(x_index, *pieces)


def place_kernel(at_ref, own_ref, other_ref, o_ref):
    x, core = at_ref[0], at_ref[1]
    for half, ref in ((core, own_ref), (1 - core, other_ref)):
        for kx in range(4):
            q = lax.rem(x + 4 - kx, 4)
            rows = pl.ds(pl.multiple_of(half * 384 + q * 96, 96), 96)
            for k in range(6):
                o_ref[rows, pl.ds(k * 128, 128)] = ref[kx, pl.ds(k * 96, 96), :]


def place_weight(at, own, other):
    return pl.pallas_call(
        place_kernel,
        in_specs=[SMEM] + [VMEM] * 2,
        out_specs=VMEM,
        out_shape=jax.ShapeDtypeStruct((D, D), BF16),
        compiler_params=params(6),
        cost_estimate=cost(),
        name="place_weight",
    )(at, own, other)


def join_kernel(core_ref, own_ref, other_ref, o_ref):
    core = core_ref[0]

    @pl.loop(0, NCHIP)
    def _(i):
        o_ref[i, core] = own_ref[i, core]
        o_ref[i, 1 - core] = other_ref[i, core]


def join_cores(core, own, other):
    return pl.pallas_call(
        join_kernel,
        in_specs=[SMEM] + [VMEM] * 2,
        out_specs=VMEM,
        out_shape=PARTS,
        compiler_params=params(10),
        cost_estimate=cost(),
        name="join_cores",
    )(core, own, other)


def right_kernel(x_index_ref, parts_ref, p_ref, l_ref, g_ref, own_ref, a_ref, b_ref, c_ref, x_ref):
    x = x_index_ref[0]

    @pl.loop(0, NCHIP)
    def _(i):
        x_ref[pl.ds(i * 2, 2)] = parts_ref[i].astype(F32)

    for k, out in enumerate((own_ref, a_ref, b_ref, c_ref)):
        a = lax.rem(x + k, 4)
        g = x_ref[:, pl.ds(pl.multiple_of(a * LJ, LJ), LJ), :].reshape(B, D).astype(BF16)
        g_ref[a] = g
        part = dot(g, p_ref[a], 1, 1).astype(out.dtype)
        for h in range(2):
            out[pl.ds(h * A, A), :] = l_ref[a * 2 + h].astype(out.dtype)
            out[pl.ds(2 * A + h * B, B), :] = part[:, h * 128:(h + 1) * 128]


def block_grads(x_index, one_parts, projected, left_part):
    rows = 2 * A + 2 * B
    return pl.pallas_call(
        right_kernel,
        in_specs=[SMEM] + [VMEM] * 3,
        out_specs=[VMEM] * 5,
        out_shape=[jax.ShapeDtypeStruct((LA, B, D), BF16), jax.ShapeDtypeStruct((rows, 128), F32)]
        + [jax.ShapeDtypeStruct((rows, 128), BF16)] * 3,
        scratch_shapes=[pltpu.VMEM((32, LA * LJ, D), F32)],
        compiler_params=params(16),
        cost_estimate=cost(),
        name="block_grads",
    )(x_index, one_parts, projected, left_part)


def back_kernel(g_ref, r_ref, w_ref, o_ref):
    proj = dot(r_ref[0], g_ref[0], 0, 0).astype(BF16)
    o_ref[0] = dot(proj, w_ref[...], 1, 1)


def back_projected(grad_one, right_blocks, in_weight):
    return pl.pallas_call(
        back_kernel,
        grid=(LA,),
        in_specs=[
            pl.BlockSpec((1, B, D), lambda a: (a, 0, 0)),
            pl.BlockSpec((1, B, B), lambda a: (a, 0, 0)),
            pl.BlockSpec((D, D), lambda a: (0, 0)),
        ],
        out_specs=pl.BlockSpec((1, B, D), lambda a: (a, 0, 0)),
        out_shape=jax.ShapeDtypeStruct((LA, B, D), F32),
        compiler_params=params(12),
        cost_estimate=cost(),
        name="back_projected",
    )(grad_one, right_blocks, in_weight)


def end_kernel(parts_ref, t_ref, g_ref, b_ref, m_ref, o_ref):
    for i in range(4):
        rows = pl.ds(i * 16, 16)
        two = parts_ref[i, pl.ds(0, 384), :].astype(F32)
        for a in range(LA):
            s = jnp.concatenate(
                [
                    jnp.concatenate([two[r + a * LJ:r + (a + 1) * LJ] for r in (k * 32, 192 + k * 32)], axis=0)
                    for k in range(6)
                ],
                axis=1,
            )
            m_ref[a, rows, :] = (s * t_ref[a, rows, :].astype(F32)).astype(BF16)
            o_ref[a, rows, :] = (g_ref[a, rows, :].astype(F32) * s + b_ref[a, rows, :]).astype(BF16)


def end(two_parts, tokens, grad_out, back_proj):
    rows = pl.BlockSpec((LA, 64, D), lambda i: (0, i, 0))
    out = jax.ShapeDtypeStruct((LA, B, D), BF16)
    return pl.pallas_call(
        end_kernel,
        grid=(4,),
        in_specs=[pl.BlockSpec((4, TWO.shape[1], 128), lambda i: (i, 0, 0)), rows, rows, rows],
        out_specs=[rows, rows],
        out_shape=[out, out],
        compiler_params=params(14),
        name="end",
    )(two_parts, tokens, grad_out, back_proj)


def exchange(v):
    return lax.all_to_all(v, CHIPS, split_axis=0, concat_axis=0, tiled=True)


def swap(v):
    return lax.ppermute(v, "c", [(0, 1), (1, 0)])


def send(v, axis, k):
    n = SIZES[axis]
    return lax.ppermute(v, axis, [(i, (i + k) % n) for i in range(n)])


def along(axis, pieces):
    return [send(v, axis, k + 1) for k, v in enumerate(pieces)]


def gather_from(v, axis):
    return jnp.stack([v] + along(axis, [v] * (SIZES[axis] - 1)))


def place_of(*axes):
    return jnp.stack([lax.axis_index(axis).astype(jnp.int32) for axis in axes])


def on_device(tokens, grad_out, right_blocks, left_blocks, in_weight):
    tokens, grad_out = tokens[0], grad_out[0]
    core, x_index = place_of("c"), place_of("x")

    grad_parts = exchange(grad_two_parts(tokens, grad_out))

    token_split, projected = front(tokens, right_blocks, in_weight)
    token_split, projected, grad_parts = lax.optimization_barrier((token_split, projected, grad_parts))
    token_parts = exchange(token_split)

    one_out, grad_j, one_j = grad_one_columns(core, grad_parts, swap(grad_parts), left_blocks)
    one_split = join_cores(core, one_out, swap(one_out))
    one_split, grad_j, one_j, token_parts = lax.optimization_barrier((one_split, grad_j, one_j, token_parts))
    one_parts = exchange(one_split)

    by_j_token, weight_mine, weight_theirs = weight_grad(core, token_parts, swap(token_parts), one_j)
    two_out, left_part = two_columns(by_j_token, in_weight, left_blocks, grad_j)
    total, *away = spread(x_index, weight_mine, swap(weight_theirs))
    two_split = join_two(core, two_out, swap(two_out), total, along("x", away))
    two_split, left_part, one_parts = lax.optimization_barrier((two_split, left_part, one_parts))
    two_parts = exchange(two_split)

    grad_one, blocks, *away = block_grads(x_index, one_parts, projected, left_part)
    got = along("x", away)
    blocks = (blocks + got[0].astype(F32)) + (got[1].astype(F32) + got[2].astype(F32))
    back_proj = back_projected(grad_one, right_blocks, in_weight)
    blocks = (blocks + send(blocks, "zl", 1)).astype(BF16)
    blocks, back_proj, two_parts = lax.optimization_barrier((blocks, back_proj, two_parts))

    weight = weight_sum(two_parts)
    weight = (weight + send(weight, "zl", 1)).astype(BF16)
    weight = exchange(jnp.broadcast_to(weight[None], (NCHIP, WCH, 128)))[:WR // WCH].reshape(WR, 128)
    grad_left, grad_right = place_blocks(x_index, [blocks] + along("x", [blocks] * 3))
    mixed, grad_tokens = end(two_parts, tokens, grad_out, back_proj)
    weight, grad_left, grad_right, mixed, grad_tokens = lax.optimization_barrier(
        (weight, grad_left, grad_right, mixed, grad_tokens)
    )
    weight = gather_from(weight, "x")
    grad_weight = place_weight(place_of("x", "c"), weight, swap(weight))
    return mixed[None], grad_tokens[None], grad_left, grad_right, grad_weight


def solution(mesh):
    fine = Mesh(mesh.devices.reshape(2, 4, 4, 4, 2), ("zl", "x", "zh", "y", "c"))
    dp, seq = ("zl", "x"), ("zh", "y", "c")
    rows = P(dp, seq, None, None)
    blocks = P(seq, None, None)
    return jax.shard_map(
        on_device,
        mesh=fine,
        in_specs=(rows, rows, blocks, blocks, P()),
        out_specs=(rows, rows, blocks, blocks, P()),
        check_vma=False,
    )
```

```python
import jax
import jax.numpy as jnp
from jax import lax
from jax.experimental import pallas as pl
from jax.experimental.pallas import tpu as pltpu
from jax.sharding import Mesh, PartitionSpec as P

F32 = jnp.float32
BF16 = jnp.bfloat16
CHIPS = ("zh", "y")
DEVICES = ("zh", "y", "c")
SIZES = {"zl": 2, "x": 4, "zh": 4, "y": 4, "c": 2}

LA, LJ, NDEV, NCHIP, A, B, D = 4, 8, 32, 16, 128, 256, 768
PARTS = jax.ShapeDtypeStruct((NDEV, LA * LJ, D), BF16)
FIRST = jax.ShapeDtypeStruct((NDEV, 2, 2, 2 * LJ, D), BF16)
WR, WCH = 576, 48
TWO = jax.ShapeDtypeStruct((NCHIP, 384 + WCH, 128), BF16)
VMEM = pl.BlockSpec(memory_space=pltpu.VMEM)
SMEM = pl.BlockSpec(memory_space=pltpu.SMEM)


def params(mib):
    return pltpu.CompilerParams(vmem_limit_bytes=mib * 1024 * 1024)


def cost(flops=1000, nbytes=1000):
    return pl.CostEstimate(flops=flops, bytes_accessed=nbytes, transcendentals=0)


def dot(a, b, ca, cb):
    return lax.dot_general(a, b, (((ca,), (cb,)), ((), ())), preferred_element_type=F32)


def first_kernel(t_ref, g_ref, r_ref, o_ref, x_ref):
    for a in range(2):
        t = t_ref[a]
        x_ref[0, a] = t.astype(F32) * g_ref[a].astype(F32)
        x_ref[1, a] = dot(r_ref[a], t, 1, 0)

    @pl.loop(0, NDEV)
    def _(i):
        rows = pl.ds(pl.multiple_of(i * LJ, LJ), LJ)
        for kind in range(2):
            both = jnp.concatenate([x_ref[kind, a, rows, :] for a in range(2)], axis=0)
            o_ref[i, 0, kind] = both.astype(BF16)


def first_parts(tokens, grad_out, right_blocks):
    rows = pl.BlockSpec((2, B, D), lambda p: (p, 0, 0))
    return pl.pallas_call(
        first_kernel,
        grid=(2,),
        in_specs=[rows, rows, pl.BlockSpec((2, B, B), lambda p: (p, 0, 0))],
        out_specs=pl.BlockSpec((NDEV, 1, 2, 2 * LJ, D), lambda p: (0, p, 0, 0, 0)),
        out_shape=FIRST,
        scratch_shapes=[pltpu.VMEM((2, 2, B, D), F32)],
        compiler_params=params(60),
        name="first_parts",
    )(tokens, grad_out, right_blocks)


def project_kernel(t_ref, w_ref, p_ref):
    for a in range(LA):
        p_ref[a] = dot(t_ref[a], w_ref[...], 1, 0).astype(BF16)


def project(tokens, in_weight):
    return pl.pallas_call(
        project_kernel,
        in_specs=[VMEM] * 2,
        out_specs=VMEM,
        out_shape=jax.ShapeDtypeStruct((LA, B, D), BF16),
        compiler_params=params(14),
        cost_estimate=cost(),
        name="project",
    )(tokens, in_weight)


COLUMNS = pltpu.VMEM((6, A * LJ, 128), F32)


def put_rows(x_ref, rows, v):
    for k in range(6):
        x_ref[k, rows, :] = v[:, k * 128:(k + 1) * 128]


def get_rows(x_ref, rows):
    return jnp.concatenate([x_ref[k, rows, :] for k in range(6)], axis=1)


def load_columns(kind, parts_ref, x_ref):
    @pl.loop(0, NDEV)
    def _(i):
        for p in range(2):
            put_rows(x_ref, pl.ds(i * 32 + p * 16, 16), parts_ref[i, p, kind].astype(F32))


def one_kernel(parts_ref, l_ref, o_ref, x_ref):
    load_columns(0, parts_ref, x_ref)
    for j in range(LJ):
        at = pl.ds(j, A, stride=LJ)
        g = get_rows(x_ref, at).astype(BF16)
        put_rows(x_ref, at, dot(l_ref[j], g, 0, 0))

    @pl.loop(0, NDEV)
    def _(i):
        o_ref[i] = get_rows(x_ref, pl.ds(i * 32, 32)).astype(BF16)


def grad_one_columns(parts, left_blocks):
    return pl.pallas_call(
        one_kernel,
        in_specs=[VMEM] * 2,
        out_specs=VMEM,
        out_shape=PARTS,
        scratch_shapes=[COLUMNS],
        compiler_params=params(18),
        cost_estimate=cost(),
        name="grad_one_columns",
    )(parts, left_blocks)


def weight_kernel(core_ref, parts_ref, l_ref, t_ref, gj_ref, mine_ref, theirs_ref, x_ref, oj_ref):
    core = core_ref[0]
    load_columns(0, parts_ref, x_ref)
    for j in range(LJ):
        g = get_rows(x_ref, pl.ds(j, A, stride=LJ)).astype(BF16)
        gj_ref[j] = g
        oj_ref[pl.ds(j * A, A), :] = dot(l_ref[j], g, 0, 0).astype(BF16)
    load_columns(1, parts_ref, x_ref)
    for j in range(LJ):
        t_ref[pl.ds(j * A, A), :] = get_rows(x_ref, pl.ds(j, A, stride=LJ)).astype(BF16)
    for half, out in ((1 - core, theirs_ref), (core, mine_ref)):
        t = t_ref[:, pl.ds(pl.multiple_of(half * 384, 128), 384)]
        part = dot(t, oj_ref[...], 0, 0)
        for q in range(4):
            for k in range(6):
                piece = part[q * 96:(q + 1) * 96, k * 128:(k + 1) * 128]
                out[q, pl.ds(k * 96, 96), :] = piece.astype(out.dtype)


def weight_grad(core, parts, left_blocks):
    half = (4, WR, 128)
    return pl.pallas_call(
        weight_kernel,
        in_specs=[SMEM] + [VMEM] * 2,
        out_specs=[VMEM] * 4,
        out_shape=[
            jax.ShapeDtypeStruct((A * LJ, D), BF16),
            jax.ShapeDtypeStruct((LJ, A, D), BF16),
            jax.ShapeDtypeStruct(half, F32),
            jax.ShapeDtypeStruct(half, BF16),
        ],
        scratch_shapes=[COLUMNS, pltpu.VMEM((A * LJ, D), BF16)],
        compiler_params=params(20),
        cost_estimate=cost(),
        name="weight_grad",
    )(core, parts, left_blocks)


def two_kernel(t_ref, w_ref, l_ref, gj_ref, o_ref, lp_ref, x_ref, s_ref):
    @pl.loop(0, 4)
    def _(i):
        rows = pl.ds(i * 256, 256)
        s_ref[rows, :] = dot(t_ref[rows, :], w_ref[...], 1, 0).astype(BF16)

    for j in range(LJ):
        v = s_ref[pl.ds(j * A, A), :]
        lp_ref[j] = dot(gj_ref[j], v, 1, 1)
        put_rows(x_ref, pl.ds(j, A, stride=LJ), dot(l_ref[j], v, 1, 0))

    @pl.loop(0, NCHIP)
    def _(i):
        for c in range(2):
            for k in range(6):
                o_ref[i, c, pl.ds(k * 32, 32), :] = x_ref[k, pl.ds(i * 64 + c * 32, 32), :].astype(BF16)


def two_columns(by_j_token, in_weight, left_blocks, by_j_grad):
    return pl.pallas_call(
        two_kernel,
        in_specs=[VMEM] * 4,
        out_specs=[VMEM] * 2,
        out_shape=[
            jax.ShapeDtypeStruct((NCHIP, 2, 192, 128), BF16),
            jax.ShapeDtypeStruct((LJ, A, A), F32),
        ],
        scratch_shapes=[COLUMNS, pltpu.VMEM((A * LJ, D), BF16)],
        compiler_params=params(18),
        cost_estimate=cost(),
        name="two_columns",
    )(by_j_token, in_weight, left_blocks, by_j_grad)


def spread_kernel(x_index_ref, mine_ref, got_ref, own_ref, *send_refs):
    x = x_index_ref[0]
    for k in range(4):
        q = lax.rem(x + k, 4)
        out = own_ref if k == 0 else send_refs[k - 1]
        out[...] = (mine_ref[q] + got_ref[q].astype(F32)).astype(out.dtype)


def spread(x_index, mine, got):
    return pl.pallas_call(
        spread_kernel,
        in_specs=[SMEM] + [VMEM] * 2,
        out_specs=[VMEM] * 4,
        out_shape=[jax.ShapeDtypeStruct((WR, 128), F32)] + [jax.ShapeDtypeStruct((WR, 128), BF16)] * 3,
        compiler_params=params(8),
        cost_estimate=cost(),
        name="spread",
    )(x_index, mine, got)


def join_two_kernel(core_ref, own_ref, other_ref, sum_ref, a_ref, b_ref, c_ref, o_ref, w_ref):
    core = core_ref[0]
    w = (sum_ref[...] + a_ref[...].astype(F32)) + (b_ref[...].astype(F32) + c_ref[...].astype(F32))
    w_ref[...] = w.astype(BF16)
    mine = pl.ds(pl.multiple_of(core * 192, 16), 192)
    theirs = pl.ds(pl.multiple_of((1 - core) * 192, 16), 192)

    @pl.loop(0, NCHIP)
    def _(i):
        o_ref[i, mine, :] = own_ref[i, core]
        o_ref[i, theirs, :] = other_ref[i, core]

    for i in range(NCHIP):
        chunk = w_ref[pl.ds(i * WCH, WCH), :] if i < WR // WCH else jnp.zeros((WCH, 128), BF16)
        o_ref[i, pl.ds(384, WCH), :] = chunk


def join_two(core, own, other, total, got):
    return pl.pallas_call(
        join_two_kernel,
        in_specs=[SMEM] + [VMEM] * 6,
        out_specs=VMEM,
        out_shape=TWO,
        scratch_shapes=[pltpu.VMEM((WR, 128), BF16)],
        compiler_params=params(14),
        cost_estimate=cost(),
        name="join_two",
    )(core, own, other, total, *got)


def weight_sum_kernel(p_ref, o_ref):
    total = p_ref[0].astype(F32)
    for i in range(1, NCHIP):
        total = total + p_ref[i].astype(F32)
    total = total.astype(BF16)
    for i in range(2 * NCHIP):
        o_ref[i] = total


def weight_sum(two_parts):
    return pl.pallas_call(
        weight_sum_kernel,
        grid=(1,),
        in_specs=[pl.BlockSpec((NCHIP, WCH, 128), lambda i: (0, 384 // WCH, 0))],
        out_specs=pl.BlockSpec((2 * NCHIP, WCH, 128), lambda i: (0, 0, 0)),
        out_shape=jax.ShapeDtypeStruct((2 * NCHIP, WCH, 128), BF16),
        compiler_params=params(6),
        cost_estimate=cost(),
        name="weight_sum",
    )(two_parts)


def blocks_kernel(x_index_ref, own_ref, a_ref, b_ref, c_ref, l_ref, r_ref):
    for k, ref in enumerate((own_ref, a_ref, b_ref, c_ref)):
        q = lax.rem(x_index_ref[0] + 4 - k, 4)
        for h in range(2):
            l_ref[q * 2 + h] = ref[pl.ds(h * A, A), :]
            r_ref[q, :, pl.ds(h * 128, 128)] = ref[pl.ds(2 * A + h * B, B), :]


def place_blocks(x_index, pieces):
    return pl.pallas_call(
        blocks_kernel,
        in_specs=[SMEM] + [VMEM] * 4,
        out_specs=[VMEM] * 2,
        out_shape=[jax.ShapeDtypeStruct((LJ, A, A), BF16), jax.ShapeDtypeStruct((LA, B, B), BF16)],
        compiler_params=params(6),
        cost_estimate=cost(),
        name="place_blocks",
    )(x_index, *pieces)


def place_kernel(at_ref, own_ref, other_ref, o_ref):
    x, core = at_ref[0], at_ref[1]
    for half, ref in ((core, own_ref), (1 - core, other_ref)):
        for kx in range(4):
            q = lax.rem(x + 4 - kx, 4)
            rows = pl.ds(pl.multiple_of(half * 384 + q * 96, 96), 96)
            for k in range(6):
                o_ref[rows, pl.ds(k * 128, 128)] = ref[kx, pl.ds(k * 96, 96), :]


def place_weight(at, own, other):
    return pl.pallas_call(
        place_kernel,
        in_specs=[SMEM] + [VMEM] * 2,
        out_specs=VMEM,
        out_shape=jax.ShapeDtypeStruct((D, D), BF16),
        compiler_params=params(6),
        cost_estimate=cost(),
        name="place_weight",
    )(at, own, other)


def right_kernel(x_index_ref, parts_ref, p_ref, l_ref, g_ref, own_ref, a_ref, b_ref, c_ref, x_ref):
    x = x_index_ref[0]

    @pl.loop(0, NDEV)
    def _(i):
        x_ref[i] = parts_ref[i].astype(F32)

    for k, out in enumerate((own_ref, a_ref, b_ref, c_ref)):
        a = lax.rem(x + k, 4)
        g = x_ref[:, pl.ds(pl.multiple_of(a * LJ, LJ), LJ), :].reshape(B, D).astype(BF16)
        g_ref[a] = g
        part = dot(g, p_ref[a], 1, 1).astype(out.dtype)
        for h in range(2):
            out[pl.ds(h * A, A), :] = l_ref[a * 2 + h].astype(out.dtype)
            out[pl.ds(2 * A + h * B, B), :] = part[:, h * 128:(h + 1) * 128]


def block_grads(x_index, one_parts, projected, left_part):
    rows = 2 * A + 2 * B
    return pl.pallas_call(
        right_kernel,
        in_specs=[SMEM] + [VMEM] * 3,
        out_specs=[VMEM] * 5,
        out_shape=[jax.ShapeDtypeStruct((LA, B, D), BF16), jax.ShapeDtypeStruct((rows, 128), F32)]
        + [jax.ShapeDtypeStruct((rows, 128), BF16)] * 3,
        scratch_shapes=[pltpu.VMEM((32, LA * LJ, D), F32)],
        compiler_params=params(16),
        cost_estimate=cost(),
        name="block_grads",
    )(x_index, one_parts, projected, left_part)


def back_kernel(g_ref, r_ref, w_ref, o_ref):
    proj = dot(r_ref[0], g_ref[0], 0, 0).astype(BF16)
    o_ref[0] = dot(proj, w_ref[...], 1, 1)


def back_projected(grad_one, right_blocks, in_weight):
    return pl.pallas_call(
        back_kernel,
        grid=(LA,),
        in_specs=[
            pl.BlockSpec((1, B, D), lambda a: (a, 0, 0)),
            pl.BlockSpec((1, B, B), lambda a: (a, 0, 0)),
            pl.BlockSpec((D, D), lambda a: (0, 0)),
        ],
        out_specs=pl.BlockSpec((1, B, D), lambda a: (a, 0, 0)),
        out_shape=jax.ShapeDtypeStruct((LA, B, D), F32),
        compiler_params=params(12),
        cost_estimate=cost(),
        name="back_projected",
    )(grad_one, right_blocks, in_weight)


def end_kernel(parts_ref, t_ref, g_ref, b_ref, m_ref, o_ref):
    for i in range(4):
        rows = pl.ds(i * 16, 16)
        two = parts_ref[i, pl.ds(0, 384), :].astype(F32)
        for a in range(LA):
            s = jnp.concatenate(
                [
                    jnp.concatenate([two[r + a * LJ:r + (a + 1) * LJ] for r in (k * 32, 192 + k * 32)], axis=0)
                    for k in range(6)
                ],
                axis=1,
            )
            m_ref[a, rows, :] = (s * t_ref[a, rows, :].astype(F32)).astype(BF16)
            o_ref[a, rows, :] = (g_ref[a, rows, :].astype(F32) * s + b_ref[a, rows, :]).astype(BF16)


def end(two_parts, tokens, grad_out, back_proj):
    rows = pl.BlockSpec((LA, 64, D), lambda i: (0, i, 0))
    out = jax.ShapeDtypeStruct((LA, B, D), BF16)
    return pl.pallas_call(
        end_kernel,
        grid=(4,),
        in_specs=[pl.BlockSpec((4, TWO.shape[1], 128), lambda i: (i, 0, 0)), rows, rows, rows],
        out_specs=[rows, rows],
        out_shape=[out, out],
        compiler_params=params(14),
        name="end",
    )(two_parts, tokens, grad_out, back_proj)


def exchange(v, axes):
    return lax.all_to_all(v, axes, split_axis=0, concat_axis=0, tiled=True)


def swap(v):
    return lax.ppermute(v, "c", [(0, 1), (1, 0)])


def send(v, axis, k):
    n = SIZES[axis]
    return lax.ppermute(v, axis, [(i, (i + k) % n) for i in range(n)])


def along(axis, pieces):
    return [send(v, axis, k + 1) for k, v in enumerate(pieces)]


def place_of(*axes):
    return jnp.stack([lax.axis_index(axis).astype(jnp.int32) for axis in axes])


def on_device(tokens, grad_out, right_blocks, left_blocks, in_weight):
    tokens, grad_out = tokens[0], grad_out[0]
    core, x_index = place_of("c"), place_of("x")

    first = exchange(first_parts(tokens, grad_out, right_blocks), DEVICES)
    projected = project(tokens, in_weight)
    first, projected = lax.optimization_barrier((first, projected))

    one_split = grad_one_columns(first, left_blocks)
    one_parts = exchange(one_split, DEVICES)

    by_j_token, grad_j, weight_mine, weight_theirs = weight_grad(core, first, left_blocks)
    two_out, left_part = two_columns(by_j_token, in_weight, left_blocks, grad_j)
    total, *away = spread(x_index, weight_mine, swap(weight_theirs))
    two_split = join_two(core, two_out, swap(two_out), total, along("x", away))
    two_split, left_part, one_parts = lax.optimization_barrier((two_split, left_part, one_parts))
    two_parts = exchange(two_split, CHIPS)

    grad_one, blocks, *away = block_grads(x_index, one_parts, projected, left_part)
    got = along("x", away)
    blocks = (blocks + got[0].astype(F32)) + (got[1].astype(F32) + got[2].astype(F32))
    back_proj = back_projected(grad_one, right_blocks, in_weight)
    blocks = blocks.astype(BF16)
    blocks = (blocks.astype(F32) + send(blocks, "zl", 1).astype(F32)).astype(BF16)
    blocks, back_proj, two_parts = lax.optimization_barrier((blocks, back_proj, two_parts))

    weight = exchange(weight_sum(two_parts), ("zl",) + CHIPS)
    grad_left, grad_right = place_blocks(x_index, [blocks] + along("x", [blocks] * 3))
    weight, two_parts, grad_left, grad_right = lax.optimization_barrier((weight, two_parts, grad_left, grad_right))
    weight = weight.reshape(2, NCHIP, WCH, 128).astype(F32)
    weight = (weight[0] + weight[1])[:WR // WCH].reshape(WR, 128).astype(BF16)
    got_weight = along("x", [weight] * 3)
    mixed, grad_tokens = end(two_parts, tokens, grad_out, back_proj)
    *got_weight, mixed, grad_tokens = lax.optimization_barrier((*got_weight, mixed, grad_tokens))
    weight = jnp.stack([weight, *got_weight])
    grad_weight = place_weight(place_of("x", "c"), weight, swap(weight))
    return mixed[None], grad_tokens[None], grad_left, grad_right, grad_weight


def solution(mesh):
    fine = Mesh(mesh.devices.reshape(2, 4, 4, 4, 2), ("zl", "x", "zh", "y", "c"))
    dp, seq = ("zl", "x"), ("zh", "y", "c")
    rows = P(dp, seq, None, None)
    blocks = P(seq, None, None)
    return jax.shard_map(
        on_device,
        mesh=fine,
        in_specs=(rows, rows, blocks, blocks, P()),
        out_specs=(rows, rows, blocks, blocks, P()),
        check_vma=False,
    )
```

```python
import jax
import jax.numpy as jnp
from jax import lax
from jax.experimental import pallas as pl
from jax.experimental.pallas import tpu as pltpu
from jax.sharding import Mesh, PartitionSpec as P

F32 = jnp.float32
BF16 = jnp.bfloat16
CHIPS = ("zh", "y")
DEVICES = ("zh", "y", "c")
SIZES = {"zl": 2, "x": 4, "zh": 4, "y": 4, "c": 2}

LA, LJ, NDEV, NCHIP, A, B, D = 4, 8, 32, 16, 128, 256, 768
PARTS = jax.ShapeDtypeStruct((NDEV, LA * LJ, D), BF16)
FIRST = jax.ShapeDtypeStruct((NDEV, 2, 2, 2 * LJ, D), BF16)
WR, WCH = 576, 48
TWO = jax.ShapeDtypeStruct((NCHIP, 384 + WCH, 128), BF16)
VMEM = pl.BlockSpec(memory_space=pltpu.VMEM)
SMEM = pl.BlockSpec(memory_space=pltpu.SMEM)


def params(mib):
    return pltpu.CompilerParams(vmem_limit_bytes=mib * 1024 * 1024)


def cost(flops=1000, nbytes=1000):
    return pl.CostEstimate(flops=flops, bytes_accessed=nbytes, transcendentals=0)


def dot(a, b, ca, cb):
    return lax.dot_general(a, b, (((ca,), (cb,)), ((), ())), preferred_element_type=F32)


def first_kernel(t_ref, g_ref, r_ref, o_ref, x_ref):
    for a in range(2):
        x_ref[a] = dot(r_ref[a], t_ref[a], 1, 0)

    @pl.loop(0, NDEV // 2, unroll=4)
    def _(i):
        rows = pl.ds(pl.multiple_of(i * 2 * LJ, 2 * LJ), 2 * LJ)
        two = [t_ref[a, rows, :].astype(F32) * g_ref[a, rows, :].astype(F32) for a in range(2)]
        one = [x_ref[a, rows, :] for a in range(2)]
        for kind, v in enumerate((two, one)):
            for h in range(2):
                both = jnp.concatenate([v[a][h * LJ:(h + 1) * LJ] for a in range(2)], axis=0)
                o_ref[i * 2 + h, 0, kind] = both.astype(BF16)


def first_parts(tokens, grad_out, right_blocks):
    rows = pl.BlockSpec((2, B, D), lambda p: (p, 0, 0))
    return pl.pallas_call(
        first_kernel,
        grid=(2,),
        in_specs=[rows, rows, pl.BlockSpec((2, B, B), lambda p: (p, 0, 0))],
        out_specs=pl.BlockSpec((NDEV, 1, 2, 2 * LJ, D), lambda p: (0, p, 0, 0, 0)),
        out_shape=FIRST,
        scratch_shapes=[pltpu.VMEM((2, B, D), F32)],
        compiler_params=params(60),
        name="first_parts",
    )(tokens, grad_out, right_blocks)


def project_kernel(t_ref, w_ref, p_ref):
    for a in range(LA):
        p_ref[a] = dot(t_ref[a], w_ref[...], 1, 0).astype(BF16)


def project(tokens, in_weight):
    return pl.pallas_call(
        project_kernel,
        in_specs=[VMEM] * 2,
        out_specs=VMEM,
        out_shape=jax.ShapeDtypeStruct((LA, B, D), BF16),
        compiler_params=params(14),
        cost_estimate=cost(),
        name="project",
    )(tokens, in_weight)


COLUMNS = pltpu.VMEM((6, A * LJ, 128), F32)


def put_rows(x_ref, rows, v):
    for k in range(6):
        x_ref[k, rows, :] = v[:, k * 128:(k + 1) * 128]


def get_rows(x_ref, rows):
    return jnp.concatenate([x_ref[k, rows, :] for k in range(6)], axis=1)


def load_columns(kind, parts_ref, x_ref):
    @pl.loop(0, NDEV, unroll=4)
    def _(i):
        for p in range(2):
            put_rows(x_ref, pl.ds(i * 32 + p * 16, 16), parts_ref[i, p, kind].astype(F32))


def one_kernel(parts_ref, l_ref, o_ref, x_ref):
    load_columns(0, parts_ref, x_ref)
    for j in range(LJ):
        at = pl.ds(j, A, stride=LJ)
        g = get_rows(x_ref, at).astype(BF16)
        put_rows(x_ref, at, dot(l_ref[j], g, 0, 0))

    @pl.loop(0, NDEV, unroll=4)
    def _(i):
        o_ref[i] = get_rows(x_ref, pl.ds(i * 32, 32)).astype(BF16)


def grad_one_columns(parts, left_blocks):
    return pl.pallas_call(
        one_kernel,
        in_specs=[VMEM] * 2,
        out_specs=VMEM,
        out_shape=PARTS,
        scratch_shapes=[COLUMNS],
        compiler_params=params(18),
        cost_estimate=cost(),
        name="grad_one_columns",
    )(parts, left_blocks)


def weight_kernel(core_ref, parts_ref, l_ref, t_ref, gj_ref, mine_ref, theirs_ref, x_ref, oj_ref):
    core = core_ref[0]
    load_columns(0, parts_ref, x_ref)
    for j in range(LJ):
        g = get_rows(x_ref, pl.ds(j, A, stride=LJ)).astype(BF16)
        gj_ref[j] = g
        oj_ref[pl.ds(j * A, A), :] = dot(l_ref[j], g, 0, 0).astype(BF16)
    load_columns(1, parts_ref, x_ref)
    for j in range(LJ):
        t_ref[pl.ds(j * A, A), :] = get_rows(x_ref, pl.ds(j, A, stride=LJ)).astype(BF16)
    for half, out in ((1 - core, theirs_ref), (core, mine_ref)):
        t = t_ref[:, pl.ds(pl.multiple_of(half * 384, 128), 384)]
        part = dot(t, oj_ref[...], 0, 0)
        for q in range(4):
            for k in range(6):
                piece = part[q * 96:(q + 1) * 96, k * 128:(k + 1) * 128]
                out[q, pl.ds(k * 96, 96), :] = piece.astype(out.dtype)


def weight_grad(core, parts, left_blocks):
    half = (4, WR, 128)
    return pl.pallas_call(
        weight_kernel,
        in_specs=[SMEM] + [VMEM] * 2,
        out_specs=[VMEM] * 4,
        out_shape=[
            jax.ShapeDtypeStruct((A * LJ, D), BF16),
            jax.ShapeDtypeStruct((LJ, A, D), BF16),
            jax.ShapeDtypeStruct(half, F32),
            jax.ShapeDtypeStruct(half, BF16),
        ],
        scratch_shapes=[COLUMNS, pltpu.VMEM((A * LJ, D), BF16)],
        compiler_params=params(20),
        cost_estimate=cost(),
        name="weight_grad",
    )(core, parts, left_blocks)


def two_kernel(t_ref, w_ref, l_ref, gj_ref, o_ref, lp_ref, x_ref, s_ref):
    @pl.loop(0, 4)
    def _(i):
        rows = pl.ds(i * 256, 256)
        s_ref[rows, :] = dot(t_ref[rows, :], w_ref[...], 1, 0).astype(BF16)

    for j in range(LJ):
        v = s_ref[pl.ds(j * A, A), :]
        lp_ref[j] = dot(gj_ref[j], v, 1, 1)
        put_rows(x_ref, pl.ds(j, A, stride=LJ), dot(l_ref[j], v, 1, 0))

    @pl.loop(0, NCHIP)
    def _(i):
        for c in range(2):
            for k in range(6):
                o_ref[i, c, pl.ds(k * 32, 32), :] = x_ref[k, pl.ds(i * 64 + c * 32, 32), :].astype(BF16)


def two_columns(by_j_token, in_weight, left_blocks, by_j_grad):
    return pl.pallas_call(
        two_kernel,
        in_specs=[VMEM] * 4,
        out_specs=[VMEM] * 2,
        out_shape=[
            jax.ShapeDtypeStruct((NCHIP, 2, 192, 128), BF16),
            jax.ShapeDtypeStruct((LJ, A, A), F32),
        ],
        scratch_shapes=[COLUMNS, pltpu.VMEM((A * LJ, D), BF16)],
        compiler_params=params(18),
        cost_estimate=cost(),
        name="two_columns",
    )(by_j_token, in_weight, left_blocks, by_j_grad)


def spread_kernel(x_index_ref, mine_ref, got_ref, own_ref, *send_refs):
    x = x_index_ref[0]
    for k in range(4):
        q = lax.rem(x + k, 4)
        out = own_ref if k == 0 else send_refs[k - 1]
        out[...] = (mine_ref[q] + got_ref[q].astype(F32)).astype(out.dtype)


def spread(x_index, mine, got):
    return pl.pallas_call(
        spread_kernel,
        in_specs=[SMEM] + [VMEM] * 2,
        out_specs=[VMEM] * 4,
        out_shape=[jax.ShapeDtypeStruct((WR, 128), F32)] + [jax.ShapeDtypeStruct((WR, 128), BF16)] * 3,
        compiler_params=params(8),
        cost_estimate=cost(),
        name="spread",
    )(x_index, mine, got)


def join_two_kernel(core_ref, own_ref, other_ref, sum_ref, a_ref, b_ref, c_ref, o_ref, w_ref):
    core = core_ref[0]
    w = (sum_ref[...] + a_ref[...].astype(F32)) + (b_ref[...].astype(F32) + c_ref[...].astype(F32))
    w_ref[...] = w.astype(BF16)
    mine = pl.ds(pl.multiple_of(core * 192, 16), 192)
    theirs = pl.ds(pl.multiple_of((1 - core) * 192, 16), 192)

    @pl.loop(0, NCHIP)
    def _(i):
        o_ref[i, mine, :] = own_ref[i, core]
        o_ref[i, theirs, :] = other_ref[i, core]

    for i in range(NCHIP):
        chunk = w_ref[pl.ds(i * WCH, WCH), :] if i < WR // WCH else jnp.zeros((WCH, 128), BF16)
        o_ref[i, pl.ds(384, WCH), :] = chunk


def join_two(core, own, other, total, got):
    return pl.pallas_call(
        join_two_kernel,
        in_specs=[SMEM] + [VMEM] * 6,
        out_specs=VMEM,
        out_shape=TWO,
        scratch_shapes=[pltpu.VMEM((WR, 128), BF16)],
        compiler_params=params(14),
        cost_estimate=cost(),
        name="join_two",
    )(core, own, other, total, *got)


def weight_sum_kernel(p_ref, o_ref):
    total = p_ref[0].astype(F32)
    for i in range(1, NCHIP):
        total = total + p_ref[i].astype(F32)
    total = total.astype(BF16)
    for i in range(2 * NCHIP):
        o_ref[i] = total


def weight_sum(two_parts):
    return pl.pallas_call(
        weight_sum_kernel,
        grid=(1,),
        in_specs=[pl.BlockSpec((NCHIP, WCH, 128), lambda i: (0, 384 // WCH, 0))],
        out_specs=pl.BlockSpec((2 * NCHIP, WCH, 128), lambda i: (0, 0, 0)),
        out_shape=jax.ShapeDtypeStruct((2 * NCHIP, WCH, 128), BF16),
        compiler_params=params(6),
        cost_estimate=cost(),
        name="weight_sum",
    )(two_parts)


def blocks_kernel(x_index_ref, own_ref, a_ref, b_ref, c_ref, l_ref, r_ref):
    for k, ref in enumerate((own_ref, a_ref, b_ref, c_ref)):
        q = lax.rem(x_index_ref[0] + 4 - k, 4)
        for h in range(2):
            l_ref[q * 2 + h] = ref[pl.ds(h * A, A), :]
            r_ref[q, :, pl.ds(h * 128, 128)] = ref[pl.ds(2 * A + h * B, B), :]


def place_blocks(x_index, pieces):
    return pl.pallas_call(
        blocks_kernel,
        in_specs=[SMEM] + [VMEM] * 4,
        out_specs=[VMEM] * 2,
        out_shape=[jax.ShapeDtypeStruct((LJ, A, A), BF16), jax.ShapeDtypeStruct((LA, B, B), BF16)],
        compiler_params=params(6),
        cost_estimate=cost(),
        name="place_blocks",
    )(x_index, *pieces)


def place_kernel(at_ref, own_ref, other_ref, o_ref):
    x, core = at_ref[0], at_ref[1]
    for half, ref in ((core, own_ref), (1 - core, other_ref)):
        for kx in range(4):
            q = lax.rem(x + 4 - kx, 4)
            rows = pl.ds(pl.multiple_of(half * 384 + q * 96, 96), 96)
            for k in range(6):
                o_ref[rows, pl.ds(k * 128, 128)] = ref[kx, pl.ds(k * 96, 96), :]


def place_weight(at, own, other):
    return pl.pallas_call(
        place_kernel,
        in_specs=[SMEM] + [VMEM] * 2,
        out_specs=VMEM,
        out_shape=jax.ShapeDtypeStruct((D, D), BF16),
        compiler_params=params(6),
        cost_estimate=cost(),
        name="place_weight",
    )(at, own, other)


def right_kernel(x_index_ref, parts_ref, p_ref, l_ref, g_ref, own_ref, a_ref, b_ref, c_ref, x_ref):
    x = x_index_ref[0]

    @pl.loop(0, NDEV)
    def _(i):
        x_ref[i] = parts_ref[i].astype(F32)

    for k, out in enumerate((own_ref, a_ref, b_ref, c_ref)):
        a = lax.rem(x + k, 4)
        g = x_ref[:, pl.ds(pl.multiple_of(a * LJ, LJ), LJ), :].reshape(B, D).astype(BF16)
        g_ref[a] = g
        part = dot(g, p_ref[a], 1, 1).astype(out.dtype)
        for h in range(2):
            out[pl.ds(h * A, A), :] = l_ref[a * 2 + h].astype(out.dtype)
            out[pl.ds(2 * A + h * B, B), :] = part[:, h * 128:(h + 1) * 128]


def block_grads(x_index, one_parts, projected, left_part):
    rows = 2 * A + 2 * B
    return pl.pallas_call(
        right_kernel,
        in_specs=[SMEM] + [VMEM] * 3,
        out_specs=[VMEM] * 5,
        out_shape=[jax.ShapeDtypeStruct((LA, B, D), BF16), jax.ShapeDtypeStruct((rows, 128), F32)]
        + [jax.ShapeDtypeStruct((rows, 128), BF16)] * 3,
        scratch_shapes=[pltpu.VMEM((32, LA * LJ, D), F32)],
        compiler_params=params(16),
        cost_estimate=cost(),
        name="block_grads",
    )(x_index, one_parts, projected, left_part)


def back_kernel(g_ref, r_ref, w_ref, o_ref):
    proj = dot(r_ref[0], g_ref[0], 0, 0).astype(BF16)
    o_ref[0] = dot(proj, w_ref[...], 1, 1)


def back_projected(grad_one, right_blocks, in_weight):
    return pl.pallas_call(
        back_kernel,
        grid=(LA,),
        in_specs=[
            pl.BlockSpec((1, B, D), lambda a: (a, 0, 0)),
            pl.BlockSpec((1, B, B), lambda a: (a, 0, 0)),
            pl.BlockSpec((D, D), lambda a: (0, 0)),
        ],
        out_specs=pl.BlockSpec((1, B, D), lambda a: (a, 0, 0)),
        out_shape=jax.ShapeDtypeStruct((LA, B, D), F32),
        compiler_params=params(12),
        cost_estimate=cost(),
        name="back_projected",
    )(grad_one, right_blocks, in_weight)


def end_kernel(parts_ref, t_ref, g_ref, b_ref, m_ref, o_ref):
    for i in range(4):
        rows = pl.ds(i * 16, 16)
        two = parts_ref[i, pl.ds(0, 384), :].astype(F32)
        for a in range(LA):
            s = jnp.concatenate(
                [
                    jnp.concatenate([two[r + a * LJ:r + (a + 1) * LJ] for r in (k * 32, 192 + k * 32)], axis=0)
                    for k in range(6)
                ],
                axis=1,
            )
            m_ref[a, rows, :] = (s * t_ref[a, rows, :].astype(F32)).astype(BF16)
            o_ref[a, rows, :] = (g_ref[a, rows, :].astype(F32) * s + b_ref[a, rows, :]).astype(BF16)


def end(two_parts, tokens, grad_out, back_proj):
    rows = pl.BlockSpec((LA, 64, D), lambda i: (0, i, 0))
    out = jax.ShapeDtypeStruct((LA, B, D), BF16)
    return pl.pallas_call(
        end_kernel,
        grid=(4,),
        in_specs=[pl.BlockSpec((4, TWO.shape[1], 128), lambda i: (i, 0, 0)), rows, rows, rows],
        out_specs=[rows, rows],
        out_shape=[out, out],
        compiler_params=params(14),
        name="end",
    )(two_parts, tokens, grad_out, back_proj)


def exchange(v, axes):
    return lax.all_to_all(v, axes, split_axis=0, concat_axis=0, tiled=True)


def swap(v):
    return lax.ppermute(v, "c", [(0, 1), (1, 0)])


def send(v, axis, k):
    n = SIZES[axis]
    return lax.ppermute(v, axis, [(i, (i + k) % n) for i in range(n)])


def along(axis, pieces):
    return [send(v, axis, k + 1) for k, v in enumerate(pieces)]


def place_of(*axes):
    return jnp.stack([lax.axis_index(axis).astype(jnp.int32) for axis in axes])


def on_device(tokens, grad_out, right_blocks, left_blocks, in_weight):
    tokens, grad_out = tokens[0], grad_out[0]
    core, x_index = place_of("c"), place_of("x")

    first = exchange(first_parts(tokens, grad_out, right_blocks), DEVICES)
    projected = project(tokens, in_weight)
    first, projected = lax.optimization_barrier((first, projected))

    one_split = grad_one_columns(first, left_blocks)
    one_parts = exchange(one_split, DEVICES)

    by_j_token, grad_j, weight_mine, weight_theirs = weight_grad(core, first, left_blocks)
    two_out, left_part = two_columns(by_j_token, in_weight, left_blocks, grad_j)
    total, *away = spread(x_index, weight_mine, swap(weight_theirs))
    two_split = join_two(core, two_out, swap(two_out), total, along("x", away))
    two_split, left_part, one_parts = lax.optimization_barrier((two_split, left_part, one_parts))
    two_parts = exchange(two_split, CHIPS)

    grad_one, blocks, *away = block_grads(x_index, one_parts, projected, left_part)
    got = along("x", away)
    blocks = (blocks + got[0].astype(F32)) + (got[1].astype(F32) + got[2].astype(F32))
    back_proj = back_projected(grad_one, right_blocks, in_weight)
    blocks = blocks.astype(BF16)
    blocks = (blocks.astype(F32) + send(blocks, "zl", 1).astype(F32)).astype(BF16)
    blocks, back_proj, two_parts = lax.optimization_barrier((blocks, back_proj, two_parts))

    weight = exchange(weight_sum(two_parts), ("zl",) + CHIPS)
    grad_left, grad_right = place_blocks(x_index, [blocks] + along("x", [blocks] * 3))
    weight, two_parts, grad_left, grad_right = lax.optimization_barrier((weight, two_parts, grad_left, grad_right))
    weight = weight.reshape(2, NCHIP, WCH, 128).astype(F32)
    weight = (weight[0] + weight[1])[:WR // WCH].reshape(WR, 128).astype(BF16)
    got_weight = along("x", [weight] * 3)
    mixed, grad_tokens = end(two_parts, tokens, grad_out, back_proj)
    *got_weight, mixed, grad_tokens = lax.optimization_barrier((*got_weight, mixed, grad_tokens))
    weight = jnp.stack([weight, *got_weight])
    grad_weight = place_weight(place_of("x", "c"), weight, swap(weight))
    return mixed[None], grad_tokens[None], grad_left, grad_right, grad_weight


def solution(mesh):
    fine = Mesh(mesh.devices.reshape(2, 4, 4, 4, 2), ("zl", "x", "zh", "y", "c"))
    dp, seq = ("zl", "x"), ("zh", "y", "c")
    rows = P(dp, seq, None, None)
    blocks = P(seq, None, None)
    return jax.shard_map(
        on_device,
        mesh=fine,
        in_specs=(rows, rows, blocks, blocks, P()),
        out_specs=(rows, rows, blocks, blocks, P()),
        check_vma=False,
    )
```

```python
import jax
import jax.numpy as jnp
from jax import lax
from jax.experimental import pallas as pl
from jax.experimental.pallas import tpu as pltpu
from jax.sharding import Mesh, PartitionSpec as P

F32 = jnp.float32
BF16 = jnp.bfloat16
CHIPS = ("zh", "y")
DEVICES = ("zh", "y", "c")
SIZES = {"zl": 2, "x": 4, "zh": 4, "y": 4, "c": 2}

LA, LJ, NDEV, NCHIP, A, B, D = 4, 8, 32, 16, 128, 256, 768
PARTS = jax.ShapeDtypeStruct((NDEV, LA * LJ, D), BF16)
FIRST = jax.ShapeDtypeStruct((NDEV, 2, 2, 2 * LJ, D), BF16)
WR, WCH = 576, 48
TWO = jax.ShapeDtypeStruct((NCHIP, 384 + WCH, 128), BF16)
VMEM = pl.BlockSpec(memory_space=pltpu.VMEM)
SMEM = pl.BlockSpec(memory_space=pltpu.SMEM)


def params(mib):
    return pltpu.CompilerParams(vmem_limit_bytes=mib * 1024 * 1024)


def cost(flops=1000, nbytes=1000):
    return pl.CostEstimate(flops=flops, bytes_accessed=nbytes, transcendentals=0)


def dot(a, b, ca, cb):
    return lax.dot_general(a, b, (((ca,), (cb,)), ((), ())), preferred_element_type=F32)


def first_kernel(t_ref, g_ref, r_ref, o_ref, x_ref):
    for a in range(2):
        x_ref[a] = dot(r_ref[a], t_ref[a], 1, 0)

    @pl.loop(0, NDEV // 2, unroll=4)
    def _(i):
        rows = pl.ds(pl.multiple_of(i * 2 * LJ, 2 * LJ), 2 * LJ)
        two = [t_ref[a, rows, :].astype(F32) * g_ref[a, rows, :].astype(F32) for a in range(2)]
        one = [x_ref[a, rows, :] for a in range(2)]
        for kind, v in enumerate((two, one)):
            for h in range(2):
                both = jnp.concatenate([v[a][h * LJ:(h + 1) * LJ] for a in range(2)], axis=0)
                o_ref[i * 2 + h, 0, kind] = both.astype(BF16)


def first_parts(tokens, grad_out, right_blocks):
    rows = pl.BlockSpec((2, B, D), lambda p: (p, 0, 0))
    return pl.pallas_call(
        first_kernel,
        grid=(2,),
        in_specs=[rows, rows, pl.BlockSpec((2, B, B), lambda p: (p, 0, 0))],
        out_specs=pl.BlockSpec((NDEV, 1, 2, 2 * LJ, D), lambda p: (0, p, 0, 0, 0)),
        out_shape=FIRST,
        scratch_shapes=[pltpu.VMEM((2, B, D), F32)],
        compiler_params=params(60),
        name="first_parts",
    )(tokens, grad_out, right_blocks)


def project_kernel(t_ref, w_ref, p_ref):
    for a in range(LA):
        p_ref[a] = dot(t_ref[a], w_ref[...], 1, 0).astype(BF16)


def project(tokens, in_weight):
    return pl.pallas_call(
        project_kernel,
        in_specs=[VMEM] * 2,
        out_specs=VMEM,
        out_shape=jax.ShapeDtypeStruct((LA, B, D), BF16),
        compiler_params=params(14),
        cost_estimate=cost(),
        name="project",
    )(tokens, in_weight)


COLUMNS = pltpu.VMEM((6, A * LJ, 128), F32)


def put_rows(x_ref, rows, v):
    for k in range(6):
        x_ref[k, rows, :] = v[:, k * 128:(k + 1) * 128]


def get_rows(x_ref, rows):
    return jnp.concatenate([x_ref[k, rows, :] for k in range(6)], axis=1)


def load_columns(kind, parts_ref, x_ref):
    @pl.loop(0, NDEV, unroll=4)
    def _(i):
        for p in range(2):
            put_rows(x_ref, pl.ds(i * 32 + p * 16, 16), parts_ref[i, p, kind].astype(F32))


def one_kernel(parts_ref, l_ref, o_ref, x_ref):
    load_columns(0, parts_ref, x_ref)
    for j in range(LJ):
        at = pl.ds(j, A, stride=LJ)
        g = get_rows(x_ref, at).astype(BF16)
        put_rows(x_ref, at, dot(l_ref[j], g, 0, 0))

    @pl.loop(0, NDEV, unroll=4)
    def _(i):
        o_ref[i] = get_rows(x_ref, pl.ds(i * 32, 32)).astype(BF16)


def grad_one_columns(parts, left_blocks):
    return pl.pallas_call(
        one_kernel,
        in_specs=[VMEM] * 2,
        out_specs=VMEM,
        out_shape=PARTS,
        scratch_shapes=[COLUMNS],
        compiler_params=params(18),
        cost_estimate=cost(),
        name="grad_one_columns",
    )(parts, left_blocks)


def weight_kernel(core_ref, parts_ref, l_ref, t_ref, gj_ref, mine_ref, theirs_ref, x_ref, oj_ref):
    core = core_ref[0]
    load_columns(0, parts_ref, x_ref)
    for j in range(LJ):
        g = get_rows(x_ref, pl.ds(j, A, stride=LJ)).astype(BF16)
        gj_ref[j] = g
        oj_ref[pl.ds(j * A, A), :] = dot(l_ref[j], g, 0, 0).astype(BF16)
    load_columns(1, parts_ref, x_ref)
    for j in range(LJ):
        t_ref[pl.ds(j * A, A), :] = get_rows(x_ref, pl.ds(j, A, stride=LJ)).astype(BF16)
    for half, out in ((1 - core, theirs_ref), (core, mine_ref)):
        t = t_ref[:, pl.ds(pl.multiple_of(half * 384, 128), 384)]
        part = dot(t, oj_ref[...], 0, 0)
        for q in range(4):
            for k in range(6):
                piece = part[q * 96:(q + 1) * 96, k * 128:(k + 1) * 128]
                out[q, pl.ds(k * 96, 96), :] = piece.astype(out.dtype)


def weight_grad(core, parts, left_blocks):
    half = (4, WR, 128)
    return pl.pallas_call(
        weight_kernel,
        in_specs=[SMEM] + [VMEM] * 2,
        out_specs=[VMEM] * 4,
        out_shape=[
            jax.ShapeDtypeStruct((A * LJ, D), BF16),
            jax.ShapeDtypeStruct((LJ, A, D), BF16),
            jax.ShapeDtypeStruct(half, F32),
            jax.ShapeDtypeStruct(half, BF16),
        ],
        scratch_shapes=[COLUMNS, pltpu.VMEM((A * LJ, D), BF16)],
        compiler_params=params(20),
        cost_estimate=cost(),
        name="weight_grad",
    )(core, parts, left_blocks)


def two_kernel(t_ref, w_ref, l_ref, gj_ref, o_ref, lp_ref, x_ref, s_ref):
    @pl.loop(0, 4)
    def _(i):
        rows = pl.ds(i * 256, 256)
        s_ref[rows, :] = dot(t_ref[rows, :], w_ref[...], 1, 0).astype(BF16)

    for j in range(LJ):
        v = s_ref[pl.ds(j * A, A), :]
        lp_ref[j] = dot(gj_ref[j], v, 1, 1)
        put_rows(x_ref, pl.ds(j, A, stride=LJ), dot(l_ref[j], v, 1, 0))

    @pl.loop(0, NCHIP)
    def _(i):
        for c in range(2):
            for k in range(6):
                o_ref[i, c, pl.ds(k * 32, 32), :] = x_ref[k, pl.ds(i * 64 + c * 32, 32), :].astype(BF16)


def two_columns(by_j_token, in_weight, left_blocks, by_j_grad):
    return pl.pallas_call(
        two_kernel,
        in_specs=[VMEM] * 4,
        out_specs=[VMEM] * 2,
        out_shape=[
            jax.ShapeDtypeStruct((NCHIP, 2, 192, 128), BF16),
            jax.ShapeDtypeStruct((LJ, A, A), F32),
        ],
        scratch_shapes=[COLUMNS, pltpu.VMEM((A * LJ, D), BF16)],
        compiler_params=params(18),
        cost_estimate=cost(),
        name="two_columns",
    )(by_j_token, in_weight, left_blocks, by_j_grad)


def spread_kernel(x_index_ref, mine_ref, got_ref, own_ref, *send_refs):
    x = x_index_ref[0]
    for k in range(4):
        q = lax.rem(x + k, 4)
        out = own_ref if k == 0 else send_refs[k - 1]
        out[...] = (mine_ref[q] + got_ref[q].astype(F32)).astype(out.dtype)


def spread(x_index, mine, got):
    return pl.pallas_call(
        spread_kernel,
        in_specs=[SMEM] + [VMEM] * 2,
        out_specs=[VMEM] * 4,
        out_shape=[jax.ShapeDtypeStruct((WR, 128), F32)] + [jax.ShapeDtypeStruct((WR, 128), BF16)] * 3,
        compiler_params=params(8),
        cost_estimate=cost(),
        name="spread",
    )(x_index, mine, got)


def join_two_kernel(core_ref, own_ref, other_ref, sum_ref, a_ref, b_ref, c_ref, o_ref, w_ref):
    core = core_ref[0]
    w = (sum_ref[...] + a_ref[...].astype(F32)) + (b_ref[...].astype(F32) + c_ref[...].astype(F32))
    w_ref[...] = w.astype(BF16)
    mine = pl.ds(pl.multiple_of(core * 192, 16), 192)
    theirs = pl.ds(pl.multiple_of((1 - core) * 192, 16), 192)

    @pl.loop(0, NCHIP)
    def _(i):
        o_ref[i, mine, :] = own_ref[i, core]
        o_ref[i, theirs, :] = other_ref[i, core]

    for i in range(NCHIP):
        chunk = w_ref[pl.ds(i * WCH, WCH), :] if i < WR // WCH else jnp.zeros((WCH, 128), BF16)
        o_ref[i, pl.ds(384, WCH), :] = chunk


def join_two(core, own, other, total, got):
    return pl.pallas_call(
        join_two_kernel,
        in_specs=[SMEM] + [VMEM] * 6,
        out_specs=VMEM,
        out_shape=TWO,
        scratch_shapes=[pltpu.VMEM((WR, 128), BF16)],
        compiler_params=params(14),
        cost_estimate=cost(),
        name="join_two",
    )(core, own, other, total, *got)


def weight_sum_kernel(p_ref, o_ref):
    total = p_ref[0].astype(F32)
    for i in range(1, NCHIP):
        total = total + p_ref[i].astype(F32)
    total = total.astype(BF16)
    for i in range(2 * NCHIP):
        o_ref[i] = total


def weight_sum(two_parts):
    return pl.pallas_call(
        weight_sum_kernel,
        grid=(1,),
        in_specs=[pl.BlockSpec((NCHIP, WCH, 128), lambda i: (0, 384 // WCH, 0))],
        out_specs=pl.BlockSpec((2 * NCHIP, WCH, 128), lambda i: (0, 0, 0)),
        out_shape=jax.ShapeDtypeStruct((2 * NCHIP, WCH, 128), BF16),
        compiler_params=params(6),
        cost_estimate=cost(),
        name="weight_sum",
    )(two_parts)


def blocks_kernel(x_index_ref, own_ref, a_ref, b_ref, c_ref, l_ref, r_ref):
    for k, ref in enumerate((own_ref, a_ref, b_ref, c_ref)):
        q = lax.rem(x_index_ref[0] + 4 - k, 4)
        for h in range(2):
            l_ref[q * 2 + h] = ref[pl.ds(h * A, A), :]
            r_ref[q, :, pl.ds(h * 128, 128)] = ref[pl.ds(2 * A + h * B, B), :]


def place_blocks(x_index, pieces):
    return pl.pallas_call(
        blocks_kernel,
        in_specs=[SMEM] + [VMEM] * 4,
        out_specs=[VMEM] * 2,
        out_shape=[jax.ShapeDtypeStruct((LJ, A, A), BF16), jax.ShapeDtypeStruct((LA, B, B), BF16)],
        compiler_params=params(6),
        cost_estimate=cost(),
        name="place_blocks",
    )(x_index, *pieces)


def place_kernel(x_index_ref, half_ref, *refs):
    pieces, o_ref = refs[:4], refs[-1]
    for kx, ref in enumerate(pieces):
        rows = pl.ds(pl.multiple_of(lax.rem(x_index_ref[0] + 4 - kx, 4) * 96, 96), 96)
        for k in range(6):
            o_ref[rows, pl.ds(k * 128, 128)] = ref[pl.ds(k * 96, 96), :]


def place_half(x_index, half, pieces, whole=None):
    rest = [] if whole is None else [whole]
    return pl.pallas_call(
        place_kernel,
        grid_spec=pltpu.PrefetchScalarGridSpec(
            num_scalar_prefetch=2,
            grid=(1,),
            in_specs=[pl.BlockSpec((WR, 128), lambda i, x, h: (0, 0))] * 4 + [pl.BlockSpec(memory_space=pl.ANY)] * len(rest),
            out_specs=pl.BlockSpec((384, D), lambda i, x, h: (h[0], 0)),
        ),
        out_shape=jax.ShapeDtypeStruct((D, D), BF16),
        input_output_aliases={} if whole is None else {6: 0},
        compiler_params=params(6),
        cost_estimate=cost(),
        name="place_half",
    )(x_index, half, *pieces, *rest)


def right_kernel(x_index_ref, parts_ref, p_ref, l_ref, g_ref, own_ref, a_ref, b_ref, c_ref, x_ref):
    x = x_index_ref[0]

    @pl.loop(0, NDEV)
    def _(i):
        x_ref[i] = parts_ref[i].astype(F32)

    for k, out in enumerate((own_ref, a_ref, b_ref, c_ref)):
        a = lax.rem(x + k, 4)
        g = x_ref[:, pl.ds(pl.multiple_of(a * LJ, LJ), LJ), :].reshape(B, D).astype(BF16)
        g_ref[a] = g
        part = dot(g, p_ref[a], 1, 1).astype(out.dtype)
        for h in range(2):
            out[pl.ds(h * A, A), :] = l_ref[a * 2 + h].astype(out.dtype)
            out[pl.ds(2 * A + h * B, B), :] = part[:, h * 128:(h + 1) * 128]


def block_grads(x_index, one_parts, projected, left_part):
    rows = 2 * A + 2 * B
    return pl.pallas_call(
        right_kernel,
        in_specs=[SMEM] + [VMEM] * 3,
        out_specs=[VMEM] * 5,
        out_shape=[jax.ShapeDtypeStruct((LA, B, D), BF16), jax.ShapeDtypeStruct((rows, 128), F32)]
        + [jax.ShapeDtypeStruct((rows, 128), BF16)] * 3,
        scratch_shapes=[pltpu.VMEM((32, LA * LJ, D), F32)],
        compiler_params=params(16),
        cost_estimate=cost(),
        name="block_grads",
    )(x_index, one_parts, projected, left_part)


def back_kernel(g_ref, r_ref, w_ref, o_ref):
    proj = dot(r_ref[0], g_ref[0], 0, 0).astype(BF16)
    o_ref[0] = dot(proj, w_ref[...], 1, 1)


def back_projected(grad_one, right_blocks, in_weight):
    return pl.pallas_call(
        back_kernel,
        grid=(LA,),
        in_specs=[
            pl.BlockSpec((1, B, D), lambda a: (a, 0, 0)),
            pl.BlockSpec((1, B, B), lambda a: (a, 0, 0)),
            pl.BlockSpec((D, D), lambda a: (0, 0)),
        ],
        out_specs=pl.BlockSpec((1, B, D), lambda a: (a, 0, 0)),
        out_shape=jax.ShapeDtypeStruct((LA, B, D), F32),
        compiler_params=params(12),
        cost_estimate=cost(),
        name="back_projected",
    )(grad_one, right_blocks, in_weight)


def end_kernel(parts_ref, t_ref, g_ref, b_ref, m_ref, o_ref):
    for i in range(4):
        rows = pl.ds(i * 16, 16)
        two = parts_ref[i, pl.ds(0, 384), :].astype(F32)
        for a in range(LA):
            s = jnp.concatenate(
                [
                    jnp.concatenate([two[r + a * LJ:r + (a + 1) * LJ] for r in (k * 32, 192 + k * 32)], axis=0)
                    for k in range(6)
                ],
                axis=1,
            )
            m_ref[a, rows, :] = (s * t_ref[a, rows, :].astype(F32)).astype(BF16)
            o_ref[a, rows, :] = (g_ref[a, rows, :].astype(F32) * s + b_ref[a, rows, :]).astype(BF16)


def end(two_parts, tokens, grad_out, back_proj):
    rows = pl.BlockSpec((LA, 64, D), lambda i: (0, i, 0))
    out = jax.ShapeDtypeStruct((LA, B, D), BF16)
    return pl.pallas_call(
        end_kernel,
        grid=(4,),
        in_specs=[pl.BlockSpec((4, TWO.shape[1], 128), lambda i: (i, 0, 0)), rows, rows, rows],
        out_specs=[rows, rows],
        out_shape=[out, out],
        compiler_params=params(14),
        name="end",
    )(two_parts, tokens, grad_out, back_proj)


def exchange(v, axes):
    return lax.all_to_all(v, axes, split_axis=0, concat_axis=0, tiled=True)


def swap(v):
    return lax.ppermute(v, "c", [(0, 1), (1, 0)])


def send(v, axis, k):
    n = SIZES[axis]
    return lax.ppermute(v, axis, [(i, (i + k) % n) for i in range(n)])


def along(axis, pieces):
    return [send(v, axis, k + 1) for k, v in enumerate(pieces)]


def place_of(*axes):
    return jnp.stack([lax.axis_index(axis).astype(jnp.int32) for axis in axes])


def on_device(tokens, grad_out, right_blocks, left_blocks, in_weight):
    tokens, grad_out = tokens[0], grad_out[0]
    core, x_index = place_of("c"), place_of("x")

    first = exchange(first_parts(tokens, grad_out, right_blocks), DEVICES)
    projected = project(tokens, in_weight)
    first, projected = lax.optimization_barrier((first, projected))

    one_split = grad_one_columns(first, left_blocks)
    one_parts = exchange(one_split, DEVICES)

    by_j_token, grad_j, weight_mine, weight_theirs = weight_grad(core, first, left_blocks)
    two_out, left_part = two_columns(by_j_token, in_weight, left_blocks, grad_j)
    total, *away = spread(x_index, weight_mine, swap(weight_theirs))
    two_split = join_two(core, two_out, swap(two_out), total, along("x", away))
    two_split, left_part, one_parts = lax.optimization_barrier((two_split, left_part, one_parts))
    two_parts = exchange(two_split, CHIPS)

    grad_one, blocks, *away = block_grads(x_index, one_parts, projected, left_part)
    got = along("x", away)
    blocks = (blocks + got[0].astype(F32)) + (got[1].astype(F32) + got[2].astype(F32))
    back_proj = back_projected(grad_one, right_blocks, in_weight)
    blocks = blocks.astype(BF16)
    blocks = (blocks.astype(F32) + send(blocks, "zl", 1).astype(F32)).astype(BF16)
    blocks, back_proj, two_parts = lax.optimization_barrier((blocks, back_proj, two_parts))

    weight = exchange(weight_sum(two_parts), ("zl",) + CHIPS)
    grad_left, grad_right = place_blocks(x_index, [blocks] + along("x", [blocks] * 3))
    weight, two_parts, grad_left, grad_right = lax.optimization_barrier((weight, two_parts, grad_left, grad_right))
    weight = weight.reshape(2, NCHIP, WCH, 128).astype(F32)
    weight = (weight[0] + weight[1])[:WR // WCH].reshape(WR, 128).astype(BF16)
    got_weight = along("x", [weight] * 3)
    mixed, grad_tokens = end(two_parts, tokens, grad_out, back_proj)
    *got_weight, mixed, grad_tokens = lax.optimization_barrier((*got_weight, mixed, grad_tokens))
    pieces = [weight, *got_weight]
    others = [swap(v) for v in pieces]
    grad_weight = place_half(x_index, core, pieces)
    *others, grad_weight = lax.optimization_barrier((*others, grad_weight))
    grad_weight = place_half(x_index, 1 - core, others, grad_weight)
    return mixed[None], grad_tokens[None], grad_left, grad_right, grad_weight


def solution(mesh):
    fine = Mesh(mesh.devices.reshape(2, 4, 4, 4, 2), ("zl", "x", "zh", "y", "c"))
    dp, seq = ("zl", "x"), ("zh", "y", "c")
    rows = P(dp, seq, None, None)
    blocks = P(seq, None, None)
    return jax.shard_map(
        on_device,
        mesh=fine,
        in_specs=(rows, rows, blocks, blocks, P()),
        out_specs=(rows, rows, blocks, blocks, P()),
        check_vma=False,
    )
```

```python
import jax
import jax.numpy as jnp
from jax import lax
from jax.experimental import pallas as pl
from jax.experimental.pallas import tpu as pltpu
from jax.sharding import Mesh, PartitionSpec as P

F32 = jnp.float32
BF16 = jnp.bfloat16
CHIPS = ("zh", "y")
DEVICES = ("zh", "y", "c")
SIZES = {"zl": 2, "x": 4, "zh": 4, "y": 4, "c": 2}

LA, LJ, NDEV, NCHIP, A, B, D = 4, 8, 32, 16, 128, 256, 768
PARTS = jax.ShapeDtypeStruct((NDEV, LA * LJ, D), BF16)
FIRST = jax.ShapeDtypeStruct((NDEV, 2, 2, 2 * LJ, D), BF16)
WR, WCH = 576, 48
TWO = jax.ShapeDtypeStruct((NCHIP, 384 + WCH, 128), BF16)
VMEM = pl.BlockSpec(memory_space=pltpu.VMEM)
SMEM = pl.BlockSpec(memory_space=pltpu.SMEM)


def params(mib):
    return pltpu.CompilerParams(vmem_limit_bytes=mib * 1024 * 1024)


def cost(flops=1000, nbytes=1000):
    return pl.CostEstimate(flops=flops, bytes_accessed=nbytes, transcendentals=0)


def dot(a, b, ca, cb):
    return lax.dot_general(a, b, (((ca,), (cb,)), ((), ())), preferred_element_type=F32)


def first_kernel(t_ref, g_ref, r_ref, o_ref, x_ref):
    for a in range(2):
        x_ref[a] = dot(r_ref[a], t_ref[a], 1, 0)

    @pl.loop(0, NDEV // 2, unroll=4)
    def _(i):
        rows = pl.ds(pl.multiple_of(i * 2 * LJ, 2 * LJ), 2 * LJ)
        two = [t_ref[a, rows, :].astype(F32) * g_ref[a, rows, :].astype(F32) for a in range(2)]
        one = [x_ref[a, rows, :] for a in range(2)]
        for kind, v in enumerate((two, one)):
            for h in range(2):
                both = jnp.concatenate([v[a][h * LJ:(h + 1) * LJ] for a in range(2)], axis=0)
                o_ref[i * 2 + h, 0, kind] = both.astype(BF16)


def first_parts(tokens, grad_out, right_blocks):
    rows = pl.BlockSpec((2, B, D), lambda p: (p, 0, 0))
    return pl.pallas_call(
        first_kernel,
        grid=(2,),
        in_specs=[rows, rows, pl.BlockSpec((2, B, B), lambda p: (p, 0, 0))],
        out_specs=pl.BlockSpec((NDEV, 1, 2, 2 * LJ, D), lambda p: (0, p, 0, 0, 0)),
        out_shape=FIRST,
        scratch_shapes=[pltpu.VMEM((2, B, D), F32)],
        compiler_params=params(60),
        name="first_parts",
    )(tokens, grad_out, right_blocks)


def project_kernel(t_ref, w_ref, p_ref):
    for a in range(LA):
        p_ref[a] = dot(t_ref[a], w_ref[...], 1, 0).astype(BF16)


def project(tokens, in_weight):
    return pl.pallas_call(
        project_kernel,
        in_specs=[VMEM] * 2,
        out_specs=VMEM,
        out_shape=jax.ShapeDtypeStruct((LA, B, D), BF16),
        compiler_params=params(14),
        cost_estimate=cost(),
        name="project",
    )(tokens, in_weight)


COLUMNS = pltpu.VMEM((6, A * LJ, 128), F32)


def put_rows(x_ref, rows, v):
    for k in range(6):
        x_ref[k, rows, :] = v[:, k * 128:(k + 1) * 128]


def get_rows(x_ref, rows):
    return jnp.concatenate([x_ref[k, rows, :] for k in range(6)], axis=1)


def load_columns(kind, parts_ref, x_ref):
    @pl.loop(0, NDEV, unroll=4)
    def _(i):
        for p in range(2):
            put_rows(x_ref, pl.ds(i * 32 + p * 16, 16), parts_ref[i, p, kind].astype(F32))


def one_kernel(parts_ref, l_ref, o_ref, x_ref):
    load_columns(0, parts_ref, x_ref)
    for j in range(LJ):
        at = pl.ds(j, A, stride=LJ)
        g = get_rows(x_ref, at).astype(BF16)
        put_rows(x_ref, at, dot(l_ref[j], g, 0, 0))

    @pl.loop(0, NDEV, unroll=4)
    def _(i):
        o_ref[i] = get_rows(x_ref, pl.ds(i * 32, 32)).astype(BF16)


def grad_one_columns(parts, left_blocks):
    return pl.pallas_call(
        one_kernel,
        in_specs=[VMEM] * 2,
        out_specs=VMEM,
        out_shape=PARTS,
        scratch_shapes=[COLUMNS],
        compiler_params=params(18),
        cost_estimate=cost(),
        name="grad_one_columns",
    )(parts, left_blocks)


def weight_kernel(core_ref, parts_ref, l_ref, t_ref, gj_ref, mine_ref, theirs_ref, x_ref, oj_ref):
    core = core_ref[0]
    load_columns(0, parts_ref, x_ref)
    for j in range(LJ):
        g = get_rows(x_ref, pl.ds(j, A, stride=LJ)).astype(BF16)
        gj_ref[j] = g
        oj_ref[pl.ds(j * A, A), :] = dot(l_ref[j], g, 0, 0).astype(BF16)
    load_columns(1, parts_ref, x_ref)
    for j in range(LJ):
        t_ref[pl.ds(j * A, A), :] = get_rows(x_ref, pl.ds(j, A, stride=LJ)).astype(BF16)
    for half, out in ((1 - core, theirs_ref), (core, mine_ref)):
        t = t_ref[:, pl.ds(pl.multiple_of(half * 384, 128), 384)]
        part = dot(t, oj_ref[...], 0, 0)
        for q in range(4):
            for k in range(6):
                piece = part[q * 96:(q + 1) * 96, k * 128:(k + 1) * 128]
                out[q, pl.ds(k * 96, 96), :] = piece.astype(out.dtype)


def weight_grad(core, parts, left_blocks):
    half = (4, WR, 128)
    return pl.pallas_call(
        weight_kernel,
        in_specs=[SMEM] + [VMEM] * 2,
        out_specs=[VMEM] * 4,
        out_shape=[
            jax.ShapeDtypeStruct((A * LJ, D), BF16),
            jax.ShapeDtypeStruct((LJ, A, D), BF16),
            jax.ShapeDtypeStruct(half, F32),
            jax.ShapeDtypeStruct(half, BF16),
        ],
        scratch_shapes=[COLUMNS, pltpu.VMEM((A * LJ, D), BF16)],
        compiler_params=params(20),
        cost_estimate=cost(),
        name="weight_grad",
    )(core, parts, left_blocks)


def two_kernel(t_ref, w_ref, l_ref, gj_ref, o_ref, lp_ref, x_ref, s_ref):
    @pl.loop(0, 4)
    def _(i):
        rows = pl.ds(i * 256, 256)
        s_ref[rows, :] = dot(t_ref[rows, :], w_ref[...], 1, 0).astype(BF16)

    for j in range(LJ):
        v = s_ref[pl.ds(j * A, A), :]
        lp_ref[j] = dot(gj_ref[j], v, 1, 1)
        put_rows(x_ref, pl.ds(j, A, stride=LJ), dot(l_ref[j], v, 1, 0))

    @pl.loop(0, NCHIP)
    def _(i):
        for c in range(2):
            for k in range(6):
                o_ref[i, c, pl.ds(k * 32, 32), :] = x_ref[k, pl.ds(i * 64 + c * 32, 32), :].astype(BF16)


def two_columns(by_j_token, in_weight, left_blocks, by_j_grad):
    return pl.pallas_call(
        two_kernel,
        in_specs=[VMEM] * 4,
        out_specs=[VMEM] * 2,
        out_shape=[
            jax.ShapeDtypeStruct((NCHIP, 2, 192, 128), BF16),
            jax.ShapeDtypeStruct((LJ, A, A), F32),
        ],
        scratch_shapes=[COLUMNS, pltpu.VMEM((A * LJ, D), BF16)],
        compiler_params=params(18),
        cost_estimate=cost(),
        name="two_columns",
    )(by_j_token, in_weight, left_blocks, by_j_grad)


def spread_kernel(x_index_ref, mine_ref, got_ref, own_ref, *send_refs):
    x = x_index_ref[0]
    for k in range(4):
        q = lax.rem(x + k, 4)
        out = own_ref if k == 0 else send_refs[k - 1]
        out[...] = (mine_ref[q] + got_ref[q].astype(F32)).astype(out.dtype)


def spread(x_index, mine, got):
    return pl.pallas_call(
        spread_kernel,
        in_specs=[SMEM] + [VMEM] * 2,
        out_specs=[VMEM] * 4,
        out_shape=[jax.ShapeDtypeStruct((WR, 128), F32)] + [jax.ShapeDtypeStruct((WR, 128), BF16)] * 3,
        compiler_params=params(8),
        cost_estimate=cost(),
        name="spread",
    )(x_index, mine, got)


def join_two_kernel(core_ref, own_ref, other_ref, sum_ref, a_ref, b_ref, c_ref, o_ref, w_ref):
    core = core_ref[0]
    w = (sum_ref[...] + a_ref[...].astype(F32)) + (b_ref[...].astype(F32) + c_ref[...].astype(F32))
    w_ref[...] = w.astype(BF16)
    mine = pl.ds(pl.multiple_of(core * 192, 16), 192)
    theirs = pl.ds(pl.multiple_of((1 - core) * 192, 16), 192)

    @pl.loop(0, NCHIP)
    def _(i):
        o_ref[i, mine, :] = own_ref[i, core]
        o_ref[i, theirs, :] = other_ref[i, core]

    for i in range(NCHIP):
        chunk = w_ref[pl.ds(i * WCH, WCH), :] if i < WR // WCH else jnp.zeros((WCH, 128), BF16)
        o_ref[i, pl.ds(384, WCH), :] = chunk


def join_two(core, own, other, total, got):
    return pl.pallas_call(
        join_two_kernel,
        in_specs=[SMEM] + [VMEM] * 6,
        out_specs=VMEM,
        out_shape=TWO,
        scratch_shapes=[pltpu.VMEM((WR, 128), BF16)],
        compiler_params=params(14),
        cost_estimate=cost(),
        name="join_two",
    )(core, own, other, total, *got)


def weight_sum_kernel(p_ref, o_ref):
    total = p_ref[0].astype(F32)
    for i in range(1, NCHIP):
        total = total + p_ref[i].astype(F32)
    total = total.astype(BF16)
    for i in range(2 * NCHIP):
        o_ref[i] = total


def weight_sum(two_parts):
    return pl.pallas_call(
        weight_sum_kernel,
        grid=(1,),
        in_specs=[pl.BlockSpec((NCHIP, WCH, 128), lambda i: (0, 384 // WCH, 0))],
        out_specs=pl.BlockSpec((2 * NCHIP, WCH, 128), lambda i: (0, 0, 0)),
        out_shape=jax.ShapeDtypeStruct((2 * NCHIP, WCH, 128), BF16),
        compiler_params=params(6),
        cost_estimate=cost(),
        name="weight_sum",
    )(two_parts)


def blocks_kernel(x_index_ref, own_ref, a_ref, b_ref, c_ref, l_ref, r_ref):
    for k, ref in enumerate((own_ref, a_ref, b_ref, c_ref)):
        q = lax.rem(x_index_ref[0] + 4 - k, 4)
        for h in range(2):
            l_ref[q * 2 + h] = ref[pl.ds(h * A, A), :]
            r_ref[q, :, pl.ds(h * 128, 128)] = ref[pl.ds(2 * A + h * B, B), :]


def place_blocks(x_index, pieces):
    return pl.pallas_call(
        blocks_kernel,
        in_specs=[SMEM] + [VMEM] * 4,
        out_specs=[VMEM] * 2,
        out_shape=[jax.ShapeDtypeStruct((LJ, A, A), BF16), jax.ShapeDtypeStruct((LA, B, B), BF16)],
        compiler_params=params(6),
        cost_estimate=cost(),
        name="place_blocks",
    )(x_index, *pieces)


def place_kernel(x_index_ref, half_ref, *refs):
    pieces, o_ref = refs[:4], refs[-1]
    for kx, ref in enumerate(pieces):
        rows = pl.ds(pl.multiple_of(lax.rem(x_index_ref[0] + 4 - kx, 4) * 96, 96), 96)
        for k in range(6):
            o_ref[rows, pl.ds(k * 128, 128)] = ref[pl.ds(k * 96, 96), :]


def place_half(x_index, half, pieces, whole=None):
    rest = [] if whole is None else [whole]
    return pl.pallas_call(
        place_kernel,
        grid_spec=pltpu.PrefetchScalarGridSpec(
            num_scalar_prefetch=2,
            grid=(1,),
            in_specs=[pl.BlockSpec((WR, 128), lambda i, x, h: (0, 0))] * 4 + [pl.BlockSpec(memory_space=pl.ANY)] * len(rest),
            out_specs=pl.BlockSpec((384, D), lambda i, x, h: (h[0], 0)),
        ),
        out_shape=jax.ShapeDtypeStruct((D, D), BF16),
        input_output_aliases={} if whole is None else {6: 0},
        compiler_params=params(6),
        cost_estimate=cost(),
        name="place_half",
    )(x_index, half, *pieces, *rest)


def right_kernel(x_index_ref, parts_ref, p_ref, l_ref, g_ref, own_ref, a_ref, b_ref, c_ref, x_ref):
    x = x_index_ref[0]

    @pl.loop(0, NDEV)
    def _(i):
        x_ref[i] = parts_ref[i].astype(F32)

    for k, out in enumerate((own_ref, a_ref, b_ref, c_ref)):
        a = lax.rem(x + k, 4)
        g = x_ref[:, pl.ds(pl.multiple_of(a * LJ, LJ), LJ), :].reshape(B, D).astype(BF16)
        g_ref[a] = g
        part = dot(g, p_ref[a], 1, 1).astype(out.dtype)
        for h in range(2):
            out[pl.ds(h * A, A), :] = l_ref[a * 2 + h].astype(out.dtype)
            out[pl.ds(2 * A + h * B, B), :] = part[:, h * 128:(h + 1) * 128]


def block_grads(x_index, one_parts, projected, left_part):
    rows = 2 * A + 2 * B
    return pl.pallas_call(
        right_kernel,
        in_specs=[SMEM] + [VMEM] * 3,
        out_specs=[VMEM] * 5,
        out_shape=[jax.ShapeDtypeStruct((LA, B, D), BF16), jax.ShapeDtypeStruct((rows, 128), F32)]
        + [jax.ShapeDtypeStruct((rows, 128), BF16)] * 3,
        scratch_shapes=[pltpu.VMEM((32, LA * LJ, D), F32)],
        compiler_params=params(16),
        cost_estimate=cost(),
        name="block_grads",
    )(x_index, one_parts, projected, left_part)


def back_kernel(g_ref, r_ref, w_ref, o_ref):
    proj = dot(r_ref[0], g_ref[0], 0, 0).astype(BF16)
    o_ref[0] = dot(proj, w_ref[...], 1, 1)


def back_projected(grad_one, right_blocks, in_weight):
    return pl.pallas_call(
        back_kernel,
        grid=(LA,),
        in_specs=[
            pl.BlockSpec((1, B, D), lambda a: (a, 0, 0)),
            pl.BlockSpec((1, B, B), lambda a: (a, 0, 0)),
            pl.BlockSpec((D, D), lambda a: (0, 0)),
        ],
        out_specs=pl.BlockSpec((1, B, D), lambda a: (a, 0, 0)),
        out_shape=jax.ShapeDtypeStruct((LA, B, D), F32),
        compiler_params=params(12),
        cost_estimate=cost(),
        name="back_projected",
    )(grad_one, right_blocks, in_weight)


def end_kernel(parts_ref, t_ref, g_ref, b_ref, m_ref, o_ref):
    for i in range(4):
        rows = pl.ds(i * 16, 16)
        two = parts_ref[i, pl.ds(0, 384), :].astype(F32)
        for a in range(LA):
            s = jnp.concatenate(
                [
                    jnp.concatenate([two[r + a * LJ:r + (a + 1) * LJ] for r in (k * 32, 192 + k * 32)], axis=0)
                    for k in range(6)
                ],
                axis=1,
            )
            m_ref[a, rows, :] = (s * t_ref[a, rows, :].astype(F32)).astype(BF16)
            o_ref[a, rows, :] = (g_ref[a, rows, :].astype(F32) * s + b_ref[a, rows, :]).astype(BF16)


def end(two_parts, tokens, grad_out, back_proj):
    rows = pl.BlockSpec((LA, 64, D), lambda i: (0, i, 0))
    out = jax.ShapeDtypeStruct((LA, B, D), BF16)
    return pl.pallas_call(
        end_kernel,
        grid=(4,),
        in_specs=[pl.BlockSpec((4, TWO.shape[1], 128), lambda i: (i, 0, 0)), rows, rows, rows],
        out_specs=[rows, rows],
        out_shape=[out, out],
        compiler_params=params(14),
        name="end",
    )(two_parts, tokens, grad_out, back_proj)


def exchange(v, axes):
    return lax.all_to_all(v, axes, split_axis=0, concat_axis=0, tiled=True)


def swap(v):
    return lax.ppermute(v, "c", [(0, 1), (1, 0)])


def send(v, axis, k):
    n = SIZES[axis]
    return lax.ppermute(v, axis, [(i, (i + k) % n) for i in range(n)])


def along(axis, pieces):
    return [send(v, axis, k + 1) for k, v in enumerate(pieces)]


def place_of(*axes):
    return jnp.stack([lax.axis_index(axis).astype(jnp.int32) for axis in axes])


def on_device(tokens, grad_out, right_blocks, left_blocks, in_weight):
    tokens, grad_out = tokens[0], grad_out[0]
    core, x_index = place_of("c"), place_of("x")

    first = exchange(first_parts(tokens, grad_out, right_blocks), DEVICES)
    projected = project(tokens, in_weight)
    first, projected = lax.optimization_barrier((first, projected))

    one_split = grad_one_columns(first, left_blocks)
    one_parts = exchange(one_split, DEVICES)

    by_j_token, grad_j, weight_mine, weight_theirs = weight_grad(core, first, left_blocks)
    two_out, left_part = two_columns(by_j_token, in_weight, left_blocks, grad_j)
    total, *away = spread(x_index, weight_mine, swap(weight_theirs))
    two_split = join_two(core, two_out, swap(two_out), total, along("x", away))
    two_split, left_part, one_parts = lax.optimization_barrier((two_split, left_part, one_parts))
    two_parts = exchange(two_split, CHIPS)

    grad_one, blocks, *away = block_grads(x_index, one_parts, projected, left_part)
    got = along("x", away)
    blocks = (blocks + got[0].astype(F32)) + (got[1].astype(F32) + got[2].astype(F32))
    back_proj = back_projected(grad_one, right_blocks, in_weight)
    blocks = blocks.astype(BF16)
    blocks = (blocks.astype(F32) + send(blocks, "zl", 1).astype(F32)).astype(BF16)
    blocks, back_proj, two_parts = lax.optimization_barrier((blocks, back_proj, two_parts))

    weight = exchange(weight_sum(two_parts), ("zh", "zl", "y"))
    grad_left, grad_right = place_blocks(x_index, [blocks] + along("x", [blocks] * 3))
    weight, two_parts, grad_left, grad_right = lax.optimization_barrier((weight, two_parts, grad_left, grad_right))
    weight = weight.reshape(4, 2, 4, WCH, 128).astype(F32)
    weight = (weight[:, 0] + weight[:, 1]).reshape(NCHIP * WCH, 128)[:WR].astype(BF16)
    got_weight = along("x", [weight] * 3)
    mixed, grad_tokens = end(two_parts, tokens, grad_out, back_proj)
    *got_weight, mixed, grad_tokens = lax.optimization_barrier((*got_weight, mixed, grad_tokens))
    pieces = [weight, *got_weight]
    others = [swap(v) for v in pieces]
    grad_weight = place_half(x_index, core, pieces)
    *others, grad_weight = lax.optimization_barrier((*others, grad_weight))
    grad_weight = place_half(x_index, 1 - core, others, grad_weight)
    return mixed[None], grad_tokens[None], grad_left, grad_right, grad_weight


def solution(mesh):
    fine = Mesh(mesh.devices.reshape(2, 4, 4, 4, 2), ("zl", "x", "zh", "y", "c"))
    dp, seq = ("zl", "x"), ("zh", "y", "c")
    rows = P(dp, seq, None, None)
    blocks = P(seq, None, None)
    return jax.shard_map(
        on_device,
        mesh=fine,
        in_specs=(rows, rows, blocks, blocks, P()),
        out_specs=(rows, rows, blocks, blocks, P()),
        check_vma=False,
    )
```

```python
import jax
import jax.numpy as jnp
from jax import lax
from jax.experimental import pallas as pl
from jax.experimental.pallas import tpu as pltpu
from jax.sharding import Mesh, PartitionSpec as P

F32 = jnp.float32
BF16 = jnp.bfloat16
CHIPS = ("zh", "y")
DEVICES = ("zh", "y", "c")
SIZES = {"zl": 2, "x": 4, "zh": 4, "y": 4, "c": 2}

LA, LJ, NDEV, NCHIP, A, B, D = 4, 8, 32, 16, 128, 256, 768
PARTS = jax.ShapeDtypeStruct((NDEV, LA * LJ, D), BF16)
FIRST = jax.ShapeDtypeStruct((NDEV, 2, 2, 2 * LJ, D), BF16)
WR, WCH = 576, 48
TWO = jax.ShapeDtypeStruct((NCHIP, 384 + WCH, 128), BF16)
VMEM = pl.BlockSpec(memory_space=pltpu.VMEM)
SMEM = pl.BlockSpec(memory_space=pltpu.SMEM)


def params(mib):
    return pltpu.CompilerParams(vmem_limit_bytes=mib * 1024 * 1024)


def cost(flops=1000, nbytes=1000):
    return pl.CostEstimate(flops=flops, bytes_accessed=nbytes, transcendentals=0)


def dot(a, b, ca, cb):
    return lax.dot_general(a, b, (((ca,), (cb,)), ((), ())), preferred_element_type=F32)


def first_kernel(t_ref, g_ref, r_ref, o_ref, x_ref):
    for a in range(2):
        x_ref[a] = dot(r_ref[a], t_ref[a], 1, 0)

    @pl.loop(0, NDEV // 2, unroll=8)
    def _(i):
        rows = pl.ds(pl.multiple_of(i * 2 * LJ, 2 * LJ), 2 * LJ)
        two = [t_ref[a, rows, :].astype(F32) * g_ref[a, rows, :].astype(F32) for a in range(2)]
        one = [x_ref[a, rows, :] for a in range(2)]
        for kind, v in enumerate((two, one)):
            for h in range(2):
                both = jnp.concatenate([v[a][h * LJ:(h + 1) * LJ] for a in range(2)], axis=0)
                o_ref[i * 2 + h, 0, kind] = both.astype(BF16)


def first_parts(tokens, grad_out, right_blocks):
    rows = pl.BlockSpec((2, B, D), lambda p: (p, 0, 0))
    return pl.pallas_call(
        first_kernel,
        grid=(2,),
        in_specs=[rows, rows, pl.BlockSpec((2, B, B), lambda p: (p, 0, 0))],
        out_specs=pl.BlockSpec((NDEV, 1, 2, 2 * LJ, D), lambda p: (0, p, 0, 0, 0)),
        out_shape=FIRST,
        scratch_shapes=[pltpu.VMEM((2, B, D), F32)],
        compiler_params=params(60),
        name="first_parts",
    )(tokens, grad_out, right_blocks)


def project_kernel(t_ref, w_ref, p_ref):
    for a in range(LA):
        p_ref[a] = dot(t_ref[a], w_ref[...], 1, 0).astype(BF16)


def project(tokens, in_weight):
    return pl.pallas_call(
        project_kernel,
        in_specs=[VMEM] * 2,
        out_specs=VMEM,
        out_shape=jax.ShapeDtypeStruct((LA, B, D), BF16),
        compiler_params=params(14),
        cost_estimate=cost(),
        name="project",
    )(tokens, in_weight)


COLUMNS = pltpu.VMEM((6, A * LJ, 128), F32)


def put_rows(x_ref, rows, v):
    for k in range(6):
        x_ref[k, rows, :] = v[:, k * 128:(k + 1) * 128]


def get_rows(x_ref, rows):
    return jnp.concatenate([x_ref[k, rows, :] for k in range(6)], axis=1)


def load_columns(kind, parts_ref, x_ref):
    @pl.loop(0, NDEV, unroll=8)
    def _(i):
        for p in range(2):
            put_rows(x_ref, pl.ds(i * 32 + p * 16, 16), parts_ref[i, p, kind].astype(F32))


def one_kernel(parts_ref, l_ref, o_ref, x_ref):
    load_columns(0, parts_ref, x_ref)
    for j in range(LJ):
        at = pl.ds(j, A, stride=LJ)
        g = get_rows(x_ref, at).astype(BF16)
        put_rows(x_ref, at, dot(l_ref[j], g, 0, 0))

    @pl.loop(0, NDEV, unroll=8)
    def _(i):
        o_ref[i] = get_rows(x_ref, pl.ds(i * 32, 32)).astype(BF16)


def grad_one_columns(parts, left_blocks):
    return pl.pallas_call(
        one_kernel,
        in_specs=[VMEM] * 2,
        out_specs=VMEM,
        out_shape=PARTS,
        scratch_shapes=[COLUMNS],
        compiler_params=params(18),
        cost_estimate=cost(),
        name="grad_one_columns",
    )(parts, left_blocks)


def weight_kernel(core_ref, parts_ref, l_ref, t_ref, gj_ref, mine_ref, theirs_ref, x_ref, oj_ref):
    core = core_ref[0]
    load_columns(0, parts_ref, x_ref)
    for j in range(LJ):
        g = get_rows(x_ref, pl.ds(j, A, stride=LJ)).astype(BF16)
        gj_ref[j] = g
        oj_ref[pl.ds(j * A, A), :] = dot(l_ref[j], g, 0, 0).astype(BF16)
    load_columns(1, parts_ref, x_ref)
    for j in range(LJ):
        t_ref[pl.ds(j * A, A), :] = get_rows(x_ref, pl.ds(j, A, stride=LJ)).astype(BF16)
    for half, out in ((1 - core, theirs_ref), (core, mine_ref)):
        t = t_ref[:, pl.ds(pl.multiple_of(half * 384, 128), 384)]
        part = dot(t, oj_ref[...], 0, 0)
        for q in range(4):
            for k in range(6):
                piece = part[q * 96:(q + 1) * 96, k * 128:(k + 1) * 128]
                out[q, pl.ds(k * 96, 96), :] = piece.astype(out.dtype)


def weight_grad(core, parts, left_blocks):
    half = (4, WR, 128)
    return pl.pallas_call(
        weight_kernel,
        in_specs=[SMEM] + [VMEM] * 2,
        out_specs=[VMEM] * 4,
        out_shape=[
            jax.ShapeDtypeStruct((A * LJ, D), BF16),
            jax.ShapeDtypeStruct((LJ, A, D), BF16),
            jax.ShapeDtypeStruct(half, F32),
            jax.ShapeDtypeStruct(half, BF16),
        ],
        scratch_shapes=[COLUMNS, pltpu.VMEM((A * LJ, D), BF16)],
        compiler_params=params(20),
        cost_estimate=cost(),
        name="weight_grad",
    )(core, parts, left_blocks)


def two_kernel(t_ref, w_ref, l_ref, gj_ref, o_ref, lp_ref, x_ref, s_ref):
    @pl.loop(0, 4)
    def _(i):
        rows = pl.ds(i * 256, 256)
        s_ref[rows, :] = dot(t_ref[rows, :], w_ref[...], 1, 0).astype(BF16)

    for j in range(LJ):
        v = s_ref[pl.ds(j * A, A), :]
        lp_ref[j] = dot(gj_ref[j], v, 1, 1)
        put_rows(x_ref, pl.ds(j, A, stride=LJ), dot(l_ref[j], v, 1, 0))

    @pl.loop(0, NCHIP)
    def _(i):
        for c in range(2):
            for k in range(6):
                o_ref[i, c, pl.ds(k * 32, 32), :] = x_ref[k, pl.ds(i * 64 + c * 32, 32), :].astype(BF16)


def two_columns(by_j_token, in_weight, left_blocks, by_j_grad):
    return pl.pallas_call(
        two_kernel,
        in_specs=[VMEM] * 4,
        out_specs=[VMEM] * 2,
        out_shape=[
            jax.ShapeDtypeStruct((NCHIP, 2, 192, 128), BF16),
            jax.ShapeDtypeStruct((LJ, A, A), F32),
        ],
        scratch_shapes=[COLUMNS, pltpu.VMEM((A * LJ, D), BF16)],
        compiler_params=params(18),
        cost_estimate=cost(),
        name="two_columns",
    )(by_j_token, in_weight, left_blocks, by_j_grad)


def spread_kernel(x_index_ref, mine_ref, got_ref, own_ref, *send_refs):
    x = x_index_ref[0]
    for k in range(4):
        q = lax.rem(x + k, 4)
        out = own_ref if k == 0 else send_refs[k - 1]
        out[...] = (mine_ref[q] + got_ref[q].astype(F32)).astype(out.dtype)


def spread(x_index, mine, got):
    return pl.pallas_call(
        spread_kernel,
        in_specs=[SMEM] + [VMEM] * 2,
        out_specs=[VMEM] * 4,
        out_shape=[jax.ShapeDtypeStruct((WR, 128), F32)] + [jax.ShapeDtypeStruct((WR, 128), BF16)] * 3,
        compiler_params=params(8),
        cost_estimate=cost(),
        name="spread",
    )(x_index, mine, got)


def join_two_kernel(core_ref, own_ref, other_ref, sum_ref, a_ref, b_ref, c_ref, o_ref, w_ref):
    core = core_ref[0]
    w = (sum_ref[...] + a_ref[...].astype(F32)) + (b_ref[...].astype(F32) + c_ref[...].astype(F32))
    w_ref[...] = w.astype(BF16)
    mine = pl.ds(pl.multiple_of(core * 192, 16), 192)
    theirs = pl.ds(pl.multiple_of((1 - core) * 192, 16), 192)

    @pl.loop(0, NCHIP)
    def _(i):
        o_ref[i, mine, :] = own_ref[i, core]
        o_ref[i, theirs, :] = other_ref[i, core]

    for i in range(NCHIP):
        chunk = w_ref[pl.ds(i * WCH, WCH), :] if i < WR // WCH else jnp.zeros((WCH, 128), BF16)
        o_ref[i, pl.ds(384, WCH), :] = chunk


def join_two(core, own, other, total, got):
    return pl.pallas_call(
        join_two_kernel,
        in_specs=[SMEM] + [VMEM] * 6,
        out_specs=VMEM,
        out_shape=TWO,
        scratch_shapes=[pltpu.VMEM((WR, 128), BF16)],
        compiler_params=params(14),
        cost_estimate=cost(),
        name="join_two",
    )(core, own, other, total, *got)


def weight_sum_kernel(p_ref, o_ref):
    total = p_ref[0].astype(F32)
    for i in range(1, NCHIP):
        total = total + p_ref[i].astype(F32)
    total = total.astype(BF16)
    for i in range(2 * NCHIP):
        o_ref[i] = total


def weight_sum(two_parts):
    return pl.pallas_call(
        weight_sum_kernel,
        grid=(1,),
        in_specs=[pl.BlockSpec((NCHIP, WCH, 128), lambda i: (0, 384 // WCH, 0))],
        out_specs=pl.BlockSpec((2 * NCHIP, WCH, 128), lambda i: (0, 0, 0)),
        out_shape=jax.ShapeDtypeStruct((2 * NCHIP, WCH, 128), BF16),
        compiler_params=params(6),
        cost_estimate=cost(),
        name="weight_sum",
    )(two_parts)


def blocks_kernel(x_index_ref, own_ref, a_ref, b_ref, c_ref, l_ref, r_ref):
    for k, ref in enumerate((own_ref, a_ref, b_ref, c_ref)):
        q = lax.rem(x_index_ref[0] + 4 - k, 4)
        for h in range(2):
            l_ref[q * 2 + h] = ref[pl.ds(h * A, A), :]
            r_ref[q, :, pl.ds(h * 128, 128)] = ref[pl.ds(2 * A + h * B, B), :]


def place_blocks(x_index, pieces):
    return pl.pallas_call(
        blocks_kernel,
        in_specs=[SMEM] + [VMEM] * 4,
        out_specs=[VMEM] * 2,
        out_shape=[jax.ShapeDtypeStruct((LJ, A, A), BF16), jax.ShapeDtypeStruct((LA, B, B), BF16)],
        compiler_params=params(6),
        cost_estimate=cost(),
        name="place_blocks",
    )(x_index, *pieces)


def place_kernel(x_index_ref, half_ref, *refs):
    pieces, o_ref = refs[:4], refs[-1]
    for kx, ref in enumerate(pieces):
        rows = pl.ds(pl.multiple_of(lax.rem(x_index_ref[0] + 4 - kx, 4) * 96, 96), 96)
        for k in range(6):
            o_ref[rows, pl.ds(k * 128, 128)] = ref[pl.ds(k * 96, 96), :]


def place_half(x_index, half, pieces, whole=None):
    rest = [] if whole is None else [whole]
    return pl.pallas_call(
        place_kernel,
        grid_spec=pltpu.PrefetchScalarGridSpec(
            num_scalar_prefetch=2,
            grid=(1,),
            in_specs=[pl.BlockSpec((WR, 128), lambda i, x, h: (0, 0))] * 4 + [pl.BlockSpec(memory_space=pl.ANY)] * len(rest),
            out_specs=pl.BlockSpec((384, D), lambda i, x, h: (h[0], 0)),
        ),
        out_shape=jax.ShapeDtypeStruct((D, D), BF16),
        input_output_aliases={} if whole is None else {6: 0},
        compiler_params=params(6),
        cost_estimate=cost(),
        name="place_half",
    )(x_index, half, *pieces, *rest)


def right_kernel(x_index_ref, parts_ref, p_ref, l_ref, g_ref, own_ref, a_ref, b_ref, c_ref, x_ref):
    x = x_index_ref[0]

    @pl.loop(0, NDEV)
    def _(i):
        x_ref[i] = parts_ref[i].astype(F32)

    for k, out in enumerate((own_ref, a_ref, b_ref, c_ref)):
        a = lax.rem(x + k, 4)
        g = x_ref[:, pl.ds(pl.multiple_of(a * LJ, LJ), LJ), :].reshape(B, D).astype(BF16)
        g_ref[a] = g
        part = dot(g, p_ref[a], 1, 1).astype(out.dtype)
        for h in range(2):
            out[pl.ds(h * A, A), :] = l_ref[a * 2 + h].astype(out.dtype)
            out[pl.ds(2 * A + h * B, B), :] = part[:, h * 128:(h + 1) * 128]


def block_grads(x_index, one_parts, projected, left_part):
    rows = 2 * A + 2 * B
    return pl.pallas_call(
        right_kernel,
        in_specs=[SMEM] + [VMEM] * 3,
        out_specs=[VMEM] * 5,
        out_shape=[jax.ShapeDtypeStruct((LA, B, D), BF16), jax.ShapeDtypeStruct((rows, 128), F32)]
        + [jax.ShapeDtypeStruct((rows, 128), BF16)] * 3,
        scratch_shapes=[pltpu.VMEM((32, LA * LJ, D), F32)],
        compiler_params=params(16),
        cost_estimate=cost(),
        name="block_grads",
    )(x_index, one_parts, projected, left_part)


def back_kernel(g_ref, r_ref, w_ref, o_ref):
    proj = dot(r_ref[0], g_ref[0], 0, 0).astype(BF16)
    o_ref[0] = dot(proj, w_ref[...], 1, 1)


def back_projected(grad_one, right_blocks, in_weight):
    return pl.pallas_call(
        back_kernel,
        grid=(LA,),
        in_specs=[
            pl.BlockSpec((1, B, D), lambda a: (a, 0, 0)),
            pl.BlockSpec((1, B, B), lambda a: (a, 0, 0)),
            pl.BlockSpec((D, D), lambda a: (0, 0)),
        ],
        out_specs=pl.BlockSpec((1, B, D), lambda a: (a, 0, 0)),
        out_shape=jax.ShapeDtypeStruct((LA, B, D), F32),
        compiler_params=params(12),
        cost_estimate=cost(),
        name="back_projected",
    )(grad_one, right_blocks, in_weight)


def end_kernel(parts_ref, t_ref, g_ref, b_ref, m_ref, o_ref):
    for i in range(4):
        rows = pl.ds(i * 16, 16)
        two = parts_ref[i, pl.ds(0, 384), :].astype(F32)
        for a in range(LA):
            s = jnp.concatenate(
                [
                    jnp.concatenate([two[r + a * LJ:r + (a + 1) * LJ] for r in (k * 32, 192 + k * 32)], axis=0)
                    for k in range(6)
                ],
                axis=1,
            )
            m_ref[a, rows, :] = (s * t_ref[a, rows, :].astype(F32)).astype(BF16)
            o_ref[a, rows, :] = (g_ref[a, rows, :].astype(F32) * s + b_ref[a, rows, :]).astype(BF16)


def end(two_parts, tokens, grad_out, back_proj):
    rows = pl.BlockSpec((LA, 64, D), lambda i: (0, i, 0))
    out = jax.ShapeDtypeStruct((LA, B, D), BF16)
    return pl.pallas_call(
        end_kernel,
        grid=(4,),
        in_specs=[pl.BlockSpec((4, TWO.shape[1], 128), lambda i: (i, 0, 0)), rows, rows, rows],
        out_specs=[rows, rows],
        out_shape=[out, out],
        compiler_params=params(14),
        name="end",
    )(two_parts, tokens, grad_out, back_proj)


def exchange(v, axes):
    return lax.all_to_all(v, axes, split_axis=0, concat_axis=0, tiled=True)


def swap(v):
    return lax.ppermute(v, "c", [(0, 1), (1, 0)])


def send(v, axis, k):
    n = SIZES[axis]
    return lax.ppermute(v, axis, [(i, (i + k) % n) for i in range(n)])


def along(axis, pieces):
    return [send(v, axis, k + 1) for k, v in enumerate(pieces)]


def place_of(*axes):
    return jnp.stack([lax.axis_index(axis).astype(jnp.int32) for axis in axes])


def on_device(tokens, grad_out, right_blocks, left_blocks, in_weight):
    tokens, grad_out = tokens[0], grad_out[0]
    core, x_index = place_of("c"), place_of("x")

    first = exchange(first_parts(tokens, grad_out, right_blocks), DEVICES)
    projected = project(tokens, in_weight)
    first, projected = lax.optimization_barrier((first, projected))

    one_split = grad_one_columns(first, left_blocks)
    one_parts = exchange(one_split, DEVICES)

    by_j_token, grad_j, weight_mine, weight_theirs = weight_grad(core, first, left_blocks)
    two_out, left_part = two_columns(by_j_token, in_weight, left_blocks, grad_j)
    total, *away = spread(x_index, weight_mine, swap(weight_theirs))
    two_split = join_two(core, two_out, swap(two_out), total, along("x", away))
    two_split, left_part, one_parts = lax.optimization_barrier((two_split, left_part, one_parts))
    two_parts = exchange(two_split, CHIPS)

    grad_one, blocks, *away = block_grads(x_index, one_parts, projected, left_part)
    got = along("x", away)
    blocks = (blocks + got[0].astype(F32)) + (got[1].astype(F32) + got[2].astype(F32))
    back_proj = back_projected(grad_one, right_blocks, in_weight)
    blocks = blocks.astype(BF16)
    blocks = (blocks.astype(F32) + send(blocks, "zl", 1).astype(F32)).astype(BF16)
    blocks, back_proj, two_parts = lax.optimization_barrier((blocks, back_proj, two_parts))

    weight = exchange(weight_sum(two_parts), ("zh", "zl", "y"))
    grad_left, grad_right = place_blocks(x_index, [blocks] + along("x", [blocks] * 3))
    weight, two_parts, grad_left, grad_right = lax.optimization_barrier((weight, two_parts, grad_left, grad_right))
    weight = weight.reshape(4, 2, 4, WCH, 128).astype(F32)
    weight = (weight[:, 0] + weight[:, 1]).reshape(NCHIP * WCH, 128)[:WR].astype(BF16)
    got_weight = along("x", [weight] * 3)
    mixed, grad_tokens = end(two_parts, tokens, grad_out, back_proj)
    *got_weight, mixed, grad_tokens = lax.optimization_barrier((*got_weight, mixed, grad_tokens))
    pieces = [weight, *got_weight]
    others = [swap(v) for v in pieces]
    grad_weight = place_half(x_index, core, pieces)
    *others, grad_weight = lax.optimization_barrier((*others, grad_weight))
    grad_weight = place_half(x_index, 1 - core, others, grad_weight)
    return mixed[None], grad_tokens[None], grad_left, grad_right, grad_weight


def solution(mesh):
    fine = Mesh(mesh.devices.reshape(2, 4, 4, 4, 2), ("zl", "x", "zh", "y", "c"))
    dp, seq = ("zl", "x"), ("zh", "y", "c")
    rows = P(dp, seq, None, None)
    blocks = P(seq, None, None)
    return jax.shard_map(
        on_device,
        mesh=fine,
        in_specs=(rows, rows, blocks, blocks, P()),
        out_specs=(rows, rows, blocks, blocks, P()),
        check_vma=False,
    )
```
